256 devices in a mesh: dp: 8 (over y, x_lo), ctx: 8 (over z), head: 4 (over x_hi, core).
Axes of the slice: x: 4 (x_hi: 2, x_lo: 2; x = x_hi * 2 + x_lo), y: 4, z: 8, core: 2. Of those that a mesh axis runs over, the one named last changes fastest.
Arguments:
- queries: bfloat16 [24576, 5120], P(('dp', 'ctx'), 'head'), parts along dimension 0, may hold values from -160 to 160
- keys: bfloat16 [24576, 1024], P(('dp', 'ctx'), 'head'), parts along dimension 0, may hold values from -8 to 8
- values: bfloat16 [24576, 1024], P(('dp', 'ctx'), 'head'), parts along dimension 0, may hold values from -6 to 6
- block_order: int32 [192], P('dp'), parts along dimension 0, may hold values from 0 to 23, as said below
- resp_lengths: int32 [128], P('dp'), parts along dimension 0, may hold values from 1 to 576, 2304 in all
Outputs:
- attended: bfloat16 [192, 128, 5120], P(('dp', 'ctx'), 'head'), parts along dimension 0
- logsumexp: float32 [40, 24576], P('head', ('dp', 'ctx')), parts along dimension 1
The draws below stay inside these ranges and needn't reach their ends.
There are 8 independent parts, one for each index of `dp`. The reference program is written for one: setup_inputs(seed, part) draws one part's arguments, and reference() takes and returns one part's arrays. A program takes and returns all parts, laid end to end along the dimension named above; each array names one. Nothing has to cross between parts.
Inputs may be any that keep to these rules, and one draw needn't show every extreme that they name: block_order is a permutation of the 24 sequence blocks; sequence blocks o * 3 to (o + 1) * 3 - 1 belong to index o of ctx, and the 3 blocks stored on one index of ctx belong to 3 different indices of ctx. `resp_lengths`: the prompt fills the first 768 positions and the 16 responses follow in order, their lengths summing to 2304.
All inputs are finite; a program needn't handle non-finite values.
Results may differ from the reference program's by a relative error of at most 0.012.
Values may be sent and summed in bfloat16 or wider, within the bound.
A program may use at most 64 MiB of HBM per device.

```python
import math
import jax
import jax.numpy as jnp
import numpy as np
from jax import lax

QUERY_HEAD_COUNT = 40
KEY_VALUE_HEADS = 8
HEAD_FEATURES = 128
MASK_BLOCK_SIZE = 128
RESP = 16
BLK_DEV = 3
QUERY_PER_KEY = 5
NBLK = 24
ROW_TOKENS = 3072
PROMPT = 768


def shared_keys(key):
    return jnp.clip(jax.random.normal(key, (ROW_TOKENS, KEY_VALUE_HEADS * HEAD_FEATURES), jnp.float32), -6.0, 6.0)


def draw_keys(key, part):
    base_offset = shared_keys(key)
    return base_offset.astype(jnp.bfloat16)


def draw_queries(key, part):
    key = jax.random.fold_in(key, 7)
    noise_key, scale_key = jax.random.split(key)
    noise = jnp.clip(jax.random.normal(noise_key, (ROW_TOKENS, QUERY_HEAD_COUNT, HEAD_FEATURES), jnp.float32), -6.0, 6.0)
    spread = jnp.exp(jax.random.uniform(scale_key, (ROW_TOKENS, QUERY_HEAD_COUNT, 1), jnp.float32, 0.0, math.log(3.5)))
    drawn = noise * spread
    return drawn.reshape(ROW_TOKENS, QUERY_HEAD_COUNT * HEAD_FEATURES).astype(jnp.bfloat16)


def draw_block_order(key, part):
    key = jax.random.fold_in(key, 3)
    shift_key, slot_key = jax.random.split(key)
    cycle_count = NBLK // BLK_DEV
    offsets = jax.random.permutation(shift_key, cycle_count)
    slot_perm = jax.random.permutation(slot_key, BLK_DEV)
    stored = jnp.arange(NBLK, dtype=jnp.int32)
    stored_dev = stored // BLK_DEV
    within = stored % BLK_DEV
    owner_dev = (stored_dev + offsets[within % cycle_count]) % cycle_count
    return (owner_dev * BLK_DEV + slot_perm[within]).astype(jnp.int32)


def levels(key, dims, pieces, smallest, top_value):
    def one(dim, shards_of):
        steps = jax.random.uniform(jax.random.fold_in(jax.random.fold_in(key, 6), dim), (shards_of,), jnp.float32, smallest / len(pieces), top_value / len(pieces))
        return jnp.repeat(jnp.exp(steps), dims[dim] // shards_of).reshape((-1,) + (1,) * (len(dims) - dim - 1))

    loudness = one(*pieces[0])
    for cut in pieces[1:]:
        loudness = loudness * one(*cut)
    return loudness


def profile(count, total, most, skew):
    weights = [(1 << 20) // math.isqrt(rank ** skew) + 1 for rank in range(2, count + 1)]
    rest, holding = total - most - (count - 1), [1] * (count - 1)
    while rest > 0:
        candidates = [i for i in range(count - 1) if holding[i] < most]
        mass, left = sum([weights[i] for i in candidates]), rest
        for i in candidates:
            more = min(most - holding[i], max(1, left * weights[i] // mass), rest)
            holding[i] = holding[i] + more
            rest = rest - more
    return np.array([most] + holding)


def uneven_parts(stream_key, number_of, total, bound, skew):
    if number_of == 2:
        one = jax.random.randint(stream_key, (), max(1, total - bound), min(bound, total - 1) + 1)
        return jnp.stack([one, total - one])
    sizes = jnp.asarray(profile(number_of, total, bound, skew), jnp.int32)
    couples = (number_of - 1) // 2
    source_of, sink = sizes[1:1 + 2 * couples:2], sizes[2:2 + 2 * couples:2]
    room = jnp.minimum(source_of - 1, bound - sink)
    passed = jax.random.randint(jax.random.fold_in(stream_key, 1), (couples,), 0, 1 << 20) % (room + 1)
    sizes = sizes.at[1:1 + 2 * couples:2].set(source_of - passed).at[2:2 + 2 * couples:2].set(sink + passed)
    return sizes[jax.random.permutation(jax.random.fold_in(stream_key, 2), number_of)]


def scatter_about(own_key, extent, width, most, shards=(), held_as=jnp.bfloat16):
    loudness = levels(own_key, extent, shards, -0.22, 0.18) if shards else 1.0
    result = jax.random.normal(own_key, extent, jnp.float32) * width * loudness
    return jnp.minimum(jnp.maximum(result, -most), most).astype(held_as)


def setup_inputs(seed: int = 0, part: int = 0) -> dict:
    arg_keys = jax.random.split(jax.random.key(seed), 6)
    part_keys = jax.random.split(jax.random.fold_in(arg_keys[5], part), 6)
    return {
        "queries": draw_queries(jax.random.fold_in(jax.random.fold_in(arg_keys[5], part), 71), part),
        "keys": draw_keys(jax.random.fold_in(jax.random.fold_in(arg_keys[5], part), 71), part),
        "values": scatter_about(part_keys[2], (ROW_TOKENS, KEY_VALUE_HEADS * HEAD_FEATURES), 1.0, 6.0, ((0, 8), (1, 4))),
        "block_order": draw_block_order(jax.random.fold_in(jax.random.fold_in(arg_keys[5], part), 71), part),
        "resp_lengths": uneven_parts(part_keys[4], RESP, ROW_TOKENS - PROMPT, (ROW_TOKENS - PROMPT) // 4, 2).astype(jnp.int32),
    }


def sequence_layout(block_order, resp_lengths):
    within = jnp.arange(MASK_BLOCK_SIZE, dtype=jnp.int32)
    position = (block_order[:, None] * MASK_BLOCK_SIZE + within[None, :]).reshape(-1).astype(jnp.int32)
    packed_row_total = position.shape[0]
    prompt = packed_row_total - jnp.sum(resp_lengths)
    resp_ends = prompt + jnp.cumsum(resp_lengths)
    later_ends = lax.optimization_barrier(jnp.sum((position[:, None] >= resp_ends[None, :]).astype(jnp.int32), axis=1))
    segment = jnp.where(position >= prompt, 1 + later_ends, 0).astype(jnp.int32)
    return (position, segment)

def reference(queries, keys, values, block_order, resp_lengths):
    position, segment = sequence_layout(block_order, resp_lengths)
    packed_row_total = queries.shape[0]
    mask_block_count = packed_row_total // MASK_BLOCK_SIZE
    query_head_tensor = queries.astype(jnp.float32).reshape(mask_block_count, MASK_BLOCK_SIZE, KEY_VALUE_HEADS, QUERY_PER_KEY, HEAD_FEATURES)
    key_head_tensor = keys.astype(jnp.float32).reshape(packed_row_total, KEY_VALUE_HEADS, HEAD_FEATURES)
    value_head_tensor = values.astype(jnp.float32).reshape(packed_row_total, KEY_VALUE_HEADS, HEAD_FEATURES)
    query_pos = position.reshape(mask_block_count, MASK_BLOCK_SIZE)
    query_seg = segment.reshape(mask_block_count, MASK_BLOCK_SIZE)

    def attend_block(packed):
        block_query, block_pos, block_seg = packed
        score = jnp.einsum('tkgd,ukd->kgtu', block_query, key_head_tensor) * (1.0 / math.sqrt(HEAD_FEATURES))
        allowed = (position[None, :] <= block_pos[:, None]) & ((segment[None, :] == 0) | (segment[None, :] == block_seg[:, None]))
        masked = jnp.where(allowed, score, -1e+30)
        row_max = lax.optimization_barrier(jnp.max(masked, axis=-1))
        raw = jnp.where(allowed, jnp.exp(masked - row_max[..., None]), 0.0)
        row_sum = lax.optimization_barrier(jnp.sum(raw, axis=-1))
        total = row_max + jnp.log(row_sum)
        normed = jnp.where(allowed, jnp.exp(masked - total[..., None]), 0.0)
        rounded = lax.optimization_barrier(normed.astype(jnp.bfloat16)).astype(jnp.float32)
        context = jnp.einsum('kgtu,ukd->kgtd', rounded, value_head_tensor, precision=lax.Precision.HIGHEST)
        return (context, total)
    context, logsumexp = lax.map(attend_block, (query_head_tensor, query_pos, query_seg))
    stored = context.transpose(0, 3, 1, 2, 4).reshape(mask_block_count, MASK_BLOCK_SIZE, QUERY_HEAD_COUNT * HEAD_FEATURES)
    inverse = jnp.zeros((mask_block_count,), jnp.int32).at[block_order].set(jnp.arange(mask_block_count, dtype=jnp.int32))
    attended = jnp.take(stored, inverse, axis=0).astype(jnp.bfloat16)
    logsumexp = logsumexp.transpose(1, 2, 0, 3).reshape(QUERY_HEAD_COUNT, packed_row_total)
    return (attended, logsumexp)
```

```python
import functools
import math

import jax
import jax.numpy as jnp
from jax import lax
from jax.experimental import pallas as pl
from jax.experimental.pallas import tpu as pltpu
from jax.sharding import PartitionSpec as P

MESH = pl.DeviceIdType.MESH
D = 128
BLK = 128
NZ = 8
NH = 4
NB = 3
GROUP = 5
SUB = BLK // NH
NBLK = NZ * NB
PROMPT_BLOCKS = 6
BAND_BLOCKS = 8
ROWS = NB * SUB
WIDTH = GROUP * D
SCALE = 1.0 / math.sqrt(D)
LOG2E = 1.4426950408889634
NEG = -1e30


def kernel(
    order_ref, resp_ref, q_ref, k_ref, v_ref, out_ref, lse_ref,
    kvbuf, kseq, vseq, qbuf, obuf, bias, lse_seq, lse_send, lse_recv, inv_ref,
    kv_send, q_send, o_send, l_send, p_send,
    kv_recv, x_recv, c_recv, f_recv, q_recv, o_recv, l_recv,
):
    z = lax.axis_index("ctx")
    h = lax.axis_index("head")
    my_k = z // 2 + 4 * lax.rem(z, 2)
    my_src = my_k // 2

    barrier = pltpu.get_barrier_semaphore()
    for dz in range(NZ):
        for e in range(NH):
            if (dz, e) != (0, 0):
                pl.semaphore_signal(
                    barrier,
                    inc=1,
                    device_id={"ctx": lax.rem(z + dz, NZ), "head": lax.rem(h + e, NH)},
                    device_id_type=MESH,
                )
    pl.semaphore_wait(barrier, NZ * NH - 1)

    def send(src, dst, send_sem, recv_sem, tz, th):
        mine = (tz == z) & (th == h)

        @pl.when(mine)
        def _():
            pltpu.make_async_copy(src, dst, recv_sem).start()

        @pl.when(jnp.logical_not(mine))
        def _():
            pltpu.make_async_remote_copy(
                src, dst, send_sem, recv_sem, device_id={"ctx": tz, "head": th}, device_id_type=MESH
            ).start()

    def sent(src, dst, send_sem, recv_sem, tz, th):
        mine = (tz == z) & (th == h)

        @pl.when(jnp.logical_not(mine))
        def _():
            pltpu.make_async_remote_copy(
                src, dst, send_sem, recv_sem, device_id={"ctx": tz, "head": th}, device_id_type=MESH
            ).wait_send()

    def landed(ref, sem):
        pltpu.make_async_copy(ref, ref, sem).wait()

    mine_blocks = pl.ds(NB * z, NB)
    kv_moves, q_moves = [], []
    for kk in range(2):
        head = 2 * h + kk
        tz = lax.rem(2 * head, NZ) + head // 4
        for r in range(NH):
            rows = pl.ds(SUB * r, SUB)
            for w, ref in enumerate((k_ref, v_ref)):
                n = (kk * NH + r) * 2 + w
                kv_moves.append((
                    ref.at[:, rows, pl.ds(D * kk, D)], kvbuf.at[r, w, mine_blocks],
                    kv_send.at[n], kv_recv, tz, r,
                ))
            q_moves.append((
                q_ref.at[:, rows, pl.ds(WIDTH * kk, WIDTH)], qbuf.at[mine_blocks],
                q_send.at[kk * NH + r], q_recv, tz, r,
            ))
    for move in kv_moves:
        send(*move)
    for move in q_moves:
        send(*move)

    def find(p, c):
        found = jnp.int32(0)
        for j in range(NBLK):
            found = jnp.where(order_ref[j] == p, j, found)
        inv_ref[p] = found
        return c

    lax.fori_loop(0, NBLK, find, 0)

    lane = lax.broadcasted_iota(jnp.int32, (ROWS, D), 1)
    row = lax.broadcasted_iota(jnp.int32, (ROWS, D), 0)
    row_pos = (row // SUB) * BLK + lax.rem(row, SUB) + SUB * h

    def band_start(o):
        return jnp.where(o < 2, 0, jnp.maximum(PROMPT_BLOCKS, NB * o - 5))

    def masks(o, c):
        q_pos = row_pos + o * (NB * BLK)
        start = jnp.full((ROWS, D), PROMPT_BLOCKS * BLK, jnp.int32)
        end = jnp.int32(PROMPT_BLOCKS * BLK)
        for n in range(resp_ref.shape[0]):
            end = end + resp_ref[n]
            start = jnp.where(q_pos >= end, end, start)
        start = jnp.where(o < 2, 0, start)
        for b in range(BAND_BLOCKS):
            key_pos = lane + (band_start(o) + b) * BLK
            allowed = (key_pos >= start) & (key_pos <= q_pos)
            bias[o, :, pl.ds(b * BLK, BLK)] = jnp.where(allowed, 0.0, NEG)
        return c

    lax.fori_loop(0, NZ, masks, 0)

    own = kvbuf.at[h]
    landed(own, kv_recv)
    x_peer = lax.rem(h + 2, NH)
    c_peer = h + 1 - 2 * lax.rem(h, 2)
    far = kvbuf.at[x_peer]
    moves = [
        (own, own, p_send.at[0], x_recv, z, x_peer),
        (own, own, p_send.at[1], c_recv, z, c_peer),
        (far, far, p_send.at[2], f_recv, z, c_peer),
    ]

    def copy(src, dst, send_sem, recv_sem, tz, th):
        return pltpu.make_async_remote_copy(
            src, dst, send_sem, recv_sem, device_id={"ctx": tz, "head": th}, device_id_type=MESH
        )

    copy(*moves[0]).start()
    copy(*moves[1]).start()
    landed(far, x_recv)
    copy(*moves[2]).start()
    landed(own, c_recv)
    landed(own, f_recv)

    def build(p, c):
        j = inv_ref[p]
        for r in range(NH):
            at = pl.ds(pl.multiple_of(p * BLK + r * SUB, SUB), SUB)
            kseq[at, :] = kvbuf[r, 0, j]
            vseq[at, :] = kvbuf[r, 1, j]
        return c

    lax.fori_loop(0, NBLK, build, 0)
    landed(qbuf, q_recv)

    def attend(o, spans):
        idx = [inv_ref[NB * o + b] for b in range(NB)]
        tile = jnp.zeros((ROWS, D), jnp.float32)
        for g in range(GROUP):
            cols = pl.ds(g * D, D)
            q = jnp.concatenate([qbuf[j, :, cols] for j in idx], axis=0)
            scores = []
            for at, use_bias in spans:
                s = lax.dot_general(
                    q, kseq[at, :], (((1,), (1,)), ((), ())), preferred_element_type=jnp.float32
                )
                if use_bias:
                    s = s + bias[o, :, pl.ds(0, s.shape[1])]
                scores.append(s)
            top = functools.reduce(jnp.maximum, [jnp.max(s, axis=1, keepdims=True) for s in scores])
            total = jnp.zeros((ROWS, 1), jnp.float32)
            acc = jnp.zeros((ROWS, D), jnp.float32)
            for (at, _), s in zip(spans, scores):
                w = jnp.exp2((s - top) * (SCALE * LOG2E))
                total = total + jnp.sum(w, axis=1, keepdims=True)
                acc = acc + jnp.dot(
                    w.astype(jnp.bfloat16), vseq[at, :], preferred_element_type=jnp.float32
                )
            res = (acc / total).astype(jnp.bfloat16)
            for b in range(NB):
                obuf[o, b, :, cols] = res[b * SUB : (b + 1) * SUB]
            tile = jnp.where(lane == g, top * SCALE + jnp.log(total), tile)
        tile = jnp.concatenate([tile, jnp.zeros((D - ROWS, D), jnp.float32)], axis=0).T[:8]
        for b in range(NB):
            lse_seq[NB * o + b] = tile if b == 0 else pltpu.roll(tile, D - SUB * b, 1)

    out_cols = pl.ds(pl.multiple_of(my_k * WIDTH, D), WIDTH)

    def o_move(o):
        return (obuf.at[o], out_ref.at[:, :, out_cols], o_send.at[o], o_recv, o, h)

    def owner(t, c):
        half = (t + 1) // 2
        o = lax.rem(z + 4 + half * (1 - 2 * lax.rem(t, 2)), NZ)

        @pl.when(o < 2)
        def _():
            attend(o, [(pl.ds(0, PROMPT_BLOCKS * BLK), True)])

        @pl.when(o >= 2)
        def _():
            first = pl.multiple_of(band_start(o) * BLK, BLK)
            attend(o, [
                (pl.ds(0, PROMPT_BLOCKS * BLK), False),
                (pl.ds(first, BAND_BLOCKS * BLK), True),
            ])

        send(*o_move(o))
        return c

    lax.fori_loop(0, NZ, owner, 0)

    lane8 = lax.broadcasted_iota(jnp.int32, (8, D), 1)

    def l_move(s):
        return (lse_send.at[s], lse_recv.at[lax.rem(my_k, 2), h], l_send.at[s], l_recv, s, my_src)

    for s in range(NZ):
        tile = lse_seq[order_ref[NB * s]]
        for b in range(1, NB):
            tile = jnp.where(
                lane8 >= SUB * b, pltpu.roll(lse_seq[order_ref[NB * s + b]], SUB * b, 1), tile
            )
        lse_send[s] = tile
        send(*l_move(s))

    landed(lse_recv, l_recv)
    for kk in range(2):
        for b in range(NB):
            tile = jnp.zeros((8, D), jnp.float32)
            for r in range(NH):
                shift = (SUB * (r - b)) % D
                part = lse_recv[kk, r]
                part = pltpu.roll(part, shift, 1) if shift else part
                tile = jnp.where(lane8 >= SUB * r, part, tile)
            lse_ref[pl.ds(kk * GROUP, GROUP), pl.ds(b * BLK, BLK)] = tile[:GROUP]

    for move in kv_moves + q_moves:
        sent(*move)
    for move in moves:
        copy(*move).wait_send()
    for s in range(NZ):
        sent(*o_move(jnp.int32(s)))
        sent(*l_move(jnp.int32(s)))
    landed(out_ref, o_recv)


def solution(mesh):
    def step(q, k, v, order, resp):
        q = q.reshape(NB, BLK, q.shape[1])
        k = k.reshape(NB, BLK, k.shape[1])
        v = v.reshape(NB, BLK, v.shape[1])
        smem = pl.BlockSpec(memory_space=pltpu.SMEM)
        hbm = pl.BlockSpec(memory_space=pl.ANY)
        vmem = pl.BlockSpec(memory_space=pltpu.VMEM)
        dma = pltpu.SemaphoreType.DMA
        return pl.pallas_call(
            kernel,
            out_shape=(
                jax.ShapeDtypeStruct((NB, SUB, NZ * WIDTH), jnp.bfloat16),
                jax.ShapeDtypeStruct((2 * GROUP, NB * BLK), jnp.float32),
            ),
            in_specs=[smem, smem, hbm, hbm, hbm],
            out_specs=(vmem, vmem),
            scratch_shapes=[
                pltpu.VMEM((NH, 2, NBLK, SUB, D), jnp.bfloat16),
                pltpu.VMEM((NBLK * BLK, D), jnp.bfloat16),
                pltpu.VMEM((NBLK * BLK, D), jnp.bfloat16),
                pltpu.VMEM((NBLK, SUB, WIDTH), jnp.bfloat16),
                pltpu.VMEM((NZ, NB, SUB, WIDTH), jnp.bfloat16),
                pltpu.VMEM((NZ, ROWS, BAND_BLOCKS * BLK), jnp.float32),
                pltpu.VMEM((NBLK, 8, D), jnp.float32),
                pltpu.VMEM((NZ, 8, D), jnp.float32),
                pltpu.VMEM((2, NH, 8, D), jnp.float32),
                pltpu.SMEM((NBLK,), jnp.int32),
                dma((4 * NH,)), dma((2 * NH,)), dma((NZ,)), dma((NZ,)), dma((3,)),
                dma, dma, dma, dma, dma, dma, dma,
            ],
            compiler_params=pltpu.CompilerParams(
                collective_id=0, has_side_effects=True, vmem_limit_bytes=44 << 20
            ),
        )(order, resp, q, k, v)

    rows = P(("dp", "ctx"), "head")
    return jax.shard_map(
        step,
        mesh=mesh,
        in_specs=(rows, rows, rows, P("dp"), P("dp")),
        out_specs=(P(("dp", "ctx"), "head", None), P("head", ("dp", "ctx"))),
        check_vma=False,
    )
```

```python
import functools
import math

import jax
import jax.numpy as jnp
from jax import lax
from jax.experimental import pallas as pl
from jax.experimental.pallas import tpu as pltpu
from jax.sharding import PartitionSpec as P

MESH = pl.DeviceIdType.MESH
D = 128
BLK = 128
NZ = 8
NH = 4
NB = 3
GROUP = 5
SUB = BLK // NH
NBLK = NZ * NB
PROMPT_BLOCKS = 6
BAND_BLOCKS = 8
ROWS = NB * SUB
WIDTH = GROUP * D
CHUNKS = ((0, 3), (3, 5))
SCALE = 1.0 / math.sqrt(D)
LOG2E = 1.4426950408889634
NEG = -1e30


def kernel(
    order_ref, resp_ref, q_ref, k_ref, v_ref, out_ref, lse_ref,
    vstage, qstage, kv, kseq, vseq, qbuf_a, qbuf_b, obuf_a, obuf_b, bias,
    lse_seq, lse_send, lse_z, lse_recv, inv_ref,
    kv_send, v_send, q1_send, q2_send, x_send, c_send, o_send, l_send, l2_send,
    v_recv, q1_recv, q2_recv, z_recv, x_recv, c_recv, o_recv, l_recv, l2_recv,
):
    z = lax.axis_index("ctx")
    h = lax.axis_index("head")
    x_peer = lax.rem(h + 2, NH)
    c_peer = h + 1 - 2 * lax.rem(h, 2)
    d_peer = lax.rem(c_peer + 2, NH)
    my_k = z // 2 + 4 * lax.rem(z, 2)
    my_src = my_k // 2
    qbuf, obuf = (qbuf_a, qbuf_b), (obuf_a, obuf_b)

    barrier = pltpu.get_barrier_semaphore()
    for dz in range(1, NZ):
        pl.semaphore_signal(
            barrier, inc=1, device_id={"ctx": lax.rem(z + dz, NZ)}, device_id_type=MESH
        )
    for th in (c_peer, x_peer, d_peer):
        pl.semaphore_signal(barrier, inc=1, device_id={"head": th}, device_id_type=MESH)
    pl.semaphore_wait(barrier, NZ - 1 + NH - 1)

    def plane(k):
        return lax.rem(2 * k, NZ) + k // 4

    def remote(src, dst, send_sem, recv_sem, tz, th):
        return pltpu.make_async_remote_copy(
            src, dst, send_sem, recv_sem, device_id={"ctx": tz, "head": th}, device_id_type=MESH
        )

    def send(src, dst, send_sem, recv_sem, tz):
        @pl.when(tz == z)
        def _():
            pltpu.make_async_copy(src, dst, recv_sem).start()

        @pl.when(tz != z)
        def _():
            remote(src, dst, send_sem, recv_sem, tz, h).start()

    def sent(src, dst, send_sem, recv_sem, tz):
        @pl.when(tz != z)
        def _():
            remote(src, dst, send_sem, recv_sem, tz, h).wait_send()

    def landed(ref, sem):
        pltpu.make_async_copy(ref, ref, sem).wait()

    here = pl.ds(NB * z, NB)

    k_moves = [
        (k_ref.at[:, :, pl.ds(D * kk, D)], kv.at[0, here], kv_send.at[kk], z_recv.at[z],
         plane(2 * h + kk))
        for kk in range(2)
    ]
    v_moves = [
        (vstage.at[:, :, pl.ds(D * kk, D)], kv.at[1, here], kv_send.at[2 + kk], z_recv.at[z],
         plane(2 * x_peer + kk))
        for kk in range(2)
    ]
    v_move = (v_ref, vstage, v_send, v_recv, z, x_peer)
    remote(*v_move).start()
    for move in k_moves:
        send(*move)

    def q_cols(c, kk):
        first, last = CHUNKS[c]
        return pl.ds(WIDTH * kk + D * first, D * (last - first))

    q1_moves = []
    for c in range(2):
        for kk in range(2):
            cols = q_cols(c, kk)
            dst = qstage.at[h, :, :, cols]
            n = 2 * c + kk
            pltpu.make_async_copy(
                q_ref.at[:, pl.ds(pl.multiple_of(SUB * h, SUB), SUB), cols], dst, q1_recv.at[n, h]
            ).start()
            for e, th in enumerate((c_peer, x_peer, d_peer)):
                rows = pl.ds(pl.multiple_of(SUB * th, SUB), SUB)
                move = (q_ref.at[:, rows, cols], dst, q1_send.at[n, e], q1_recv.at[n, h], z, th)
                remote(*move).start()
                q1_moves.append(move)

    q2_moves = []

    def forward(c):
        for e, hd in enumerate((h, c_peer, x_peer, d_peer)):
            for kk in range(2):
                src = qstage.at[hd, :, :, q_cols(c, kk)]
                move = (
                    src, qbuf[c].at[here], q2_send.at[c, 2 * e + kk], q2_recv.at[c],
                    plane(2 * hd + kk),
                )
                landed(src, q1_recv.at[2 * c + kk, hd])
                send(*move)
                q2_moves.append(move)

    landed(vstage, v_recv)
    for move in v_moves:
        send(*move)
    forward(0)

    primary = lax.rem(h, 2) == lax.rem(my_src, 2)
    which = lax.rem(h // 2 + my_src // 2, 2)

    def piece(w, s):
        return kv.at[w, pl.ds(NB * s, NB)]

    def x_move(s):
        src = piece(which, s)
        return (src, src, x_send.at[s], x_recv.at[s], z, x_peer)

    def c_move(w, s):
        src = piece(w, s)
        return (src, src, c_send.at[w, s], c_recv, z, c_peer)

    def source(t):
        return lax.rem(z + 4 + ((t + 1) // 2) * (1 - 2 * lax.rem(t, 2)), NZ)

    @pl.when(primary)
    def _():
        def own(t, c):
            s = source(NZ - 1 - t)
            landed(piece(which, s), z_recv.at[s])
            remote(*x_move(s)).start()
            remote(*c_move(which, s)).start()
            return c

        lax.fori_loop(0, NZ, own, 0)

    forward(1)

    def find(p, c):
        found = jnp.int32(0)
        for j in range(NBLK):
            found = jnp.where(order_ref[j] == p, j, found)
        inv_ref[p] = found
        return c

    lax.fori_loop(0, NBLK, find, 0)

    lane = lax.broadcasted_iota(jnp.int32, (ROWS, D), 1)
    row = lax.broadcasted_iota(jnp.int32, (ROWS, D), 0)
    row_pos = (row // SUB) * BLK + lax.rem(row, SUB) + SUB * h

    def band_start(o):
        return jnp.where(o < 2, 0, jnp.maximum(PROMPT_BLOCKS, NB * o - 5))

    def masks(o, c):
        q_pos = row_pos + o * (NB * BLK)
        start = jnp.full((ROWS, D), PROMPT_BLOCKS * BLK, jnp.int32)
        end = jnp.int32(PROMPT_BLOCKS * BLK)
        for n in range(resp_ref.shape[0]):
            end = end + resp_ref[n]
            start = jnp.where(q_pos >= end, end, start)
        start = jnp.where(o < 2, 0, start)
        for b in range(BAND_BLOCKS):
            key_pos = lane + (band_start(o) + b) * BLK
            allowed = (key_pos >= start) & (key_pos <= q_pos)
            bias[o, :, pl.ds(b * BLK, BLK)] = jnp.where(allowed, 0.0, NEG)
        return c

    lax.fori_loop(0, NZ, masks, 0)

    @pl.when(primary)
    def _():
        def other(t, c):
            s = source(NZ - 1 - t)
            landed(piece(1 - which, s), x_recv.at[s])
            remote(*c_move(1 - which, s)).start()
            return c

        lax.fori_loop(0, NZ, other, 0)

    @pl.when(jnp.logical_not(primary))
    def _():
        landed(kv, c_recv)

    def build(p, c):
        j = inv_ref[p]
        at = pl.ds(pl.multiple_of(p * BLK, BLK), BLK)
        kseq[at, :] = kv[0, j]
        vseq[at, :] = kv[1, j]
        return c

    lax.fori_loop(0, NBLK, build, 0)

    def attend(c, o, spans):
        idx = [inv_ref[NB * o + b] for b in range(NB)]
        tile = jnp.zeros((ROWS, D), jnp.float32)
        for g in range(*CHUNKS[c]):
            cols = pl.ds((g - CHUNKS[c][0]) * D, D)
            q = jnp.concatenate([qbuf[c][j, :, cols] for j in idx], axis=0)
            scores = []
            for at, use_bias in spans:
                s = lax.dot_general(
                    q, kseq[at, :], (((1,), (1,)), ((), ())), preferred_element_type=jnp.float32
                )
                if use_bias:
                    s = s + bias[o, :, pl.ds(0, s.shape[1])]
                scores.append(s)
            top = functools.reduce(jnp.maximum, [jnp.max(s, axis=1, keepdims=True) for s in scores])
            total = jnp.zeros((ROWS, 1), jnp.float32)
            acc = jnp.zeros((ROWS, D), jnp.float32)
            for (at, _), s in zip(spans, scores):
                w = jnp.exp2((s - top) * (SCALE * LOG2E))
                total = total + jnp.sum(w, axis=1, keepdims=True)
                acc = acc + jnp.dot(
                    w.astype(jnp.bfloat16), vseq[at, :], preferred_element_type=jnp.float32
                )
            res = (acc / total).astype(jnp.bfloat16)
            for b in range(NB):
                obuf[c][o, b, :, cols] = res[b * SUB : (b + 1) * SUB]
            tile = jnp.where(lane == g, top * SCALE + jnp.log(total), tile)
        tile = jnp.concatenate([tile, jnp.zeros((D - ROWS, D), jnp.float32)], axis=0).T[:8]
        for b in range(NB):
            part = tile if b == 0 else pltpu.roll(tile, D - SUB * b, 1)
            lse_seq[NB * o + b] = part if c == 0 else part + lse_seq[NB * o + b]

    def o_move(c, o):
        first, last = CHUNKS[c]
        cols = pl.ds(pl.multiple_of(my_k * WIDTH + first * D, D), (last - first) * D)
        return (obuf[c].at[o], out_ref.at[:, :, cols], o_send.at[c, o], o_recv, o)

    for c in range(2):
        landed(qbuf[c], q2_recv.at[c])

        def owner(t, carry, c=c):
            o = source(t)

            @pl.when(o < 2)
            def _():
                attend(c, o, [(pl.ds(0, PROMPT_BLOCKS * BLK), True)])

            @pl.when(o >= 2)
            def _():
                first = pl.multiple_of(band_start(o) * BLK, BLK)
                attend(c, o, [
                    (pl.ds(0, PROMPT_BLOCKS * BLK), False),
                    (pl.ds(first, BAND_BLOCKS * BLK), True),
                ])

            send(*o_move(c, o))
            return carry

        lax.fori_loop(0, NZ, owner, 0)

    lane8 = lax.broadcasted_iota(jnp.int32, (8, D), 1)

    def l_move(s):
        return (lse_send.at[s], lse_z.at[my_k], l_send.at[s], l_recv, s)

    def l2_move(e, th):
        return (lse_z.at[pl.ds(2 * th, 2)], lse_recv.at[h], l2_send.at[e], l2_recv, z, th)

    for s in range(NZ):
        tile = lse_seq[order_ref[NB * s]]
        for b in range(1, NB):
            tile = jnp.where(
                lane8 >= SUB * b, pltpu.roll(lse_seq[order_ref[NB * s + b]], SUB * b, 1), tile
            )
        lse_send[s] = tile
        send(*l_move(s))

    landed(lse_z, l_recv)
    pltpu.make_async_copy(lse_z.at[pl.ds(2 * h, 2)], lse_recv.at[h], l2_recv).start()
    for e, th in enumerate((c_peer, x_peer, d_peer)):
        remote(*l2_move(e, th)).start()
    landed(lse_recv, l2_recv)
    for kk in range(2):
        for b in range(NB):
            tile = jnp.zeros((8, D), jnp.float32)
            for r in range(NH):
                shift = (SUB * (r - b)) % D
                part = lse_recv[r, kk]
                part = pltpu.roll(part, shift, 1) if shift else part
                tile = jnp.where(lane8 >= SUB * r, part, tile)
            lse_ref[pl.ds(kk * GROUP, GROUP), pl.ds(b * BLK, BLK)] = tile[:GROUP]

    remote(*v_move).wait_send()
    for move in k_moves + v_moves + q2_moves:
        sent(*move)
    for move in q1_moves:
        remote(*move).wait_send()
    for e, th in enumerate((c_peer, x_peer, d_peer)):
        remote(*l2_move(e, th)).wait_send()

    @pl.when(primary)
    def _():
        def done(s, c):
            remote(*x_move(s)).wait_send()
            remote(*c_move(0, s)).wait_send()
            remote(*c_move(1, s)).wait_send()
            return c

        lax.fori_loop(0, NZ, done, 0)

    for s in range(NZ):
        sent(*l_move(jnp.int32(s)))
        for c in range(2):
            sent(*o_move(c, jnp.int32(s)))
    landed(out_ref, o_recv)


def solution(mesh):
    def step(q, k, v, order, resp):
        q = q.reshape(NB, BLK, q.shape[1])
        k = k.reshape(NB, BLK, k.shape[1])
        v = v.reshape(NB, BLK, v.shape[1])
        smem = pl.BlockSpec(memory_space=pltpu.SMEM)
        hbm = pl.BlockSpec(memory_space=pl.ANY)
        vmem = pl.BlockSpec(memory_space=pltpu.VMEM)
        dma = pltpu.SemaphoreType.DMA
        bf16 = lambda *shape: pltpu.VMEM(shape, jnp.bfloat16)
        f32 = lambda *shape: pltpu.VMEM(shape, jnp.float32)
        widths = [D * (last - first) for first, last in CHUNKS]
        return pl.pallas_call(
            kernel,
            out_shape=(
                jax.ShapeDtypeStruct((NB, SUB, NZ * WIDTH), jnp.bfloat16),
                jax.ShapeDtypeStruct((2 * GROUP, NB * BLK), jnp.float32),
            ),
            in_specs=[smem, smem, hbm, hbm, hbm],
            out_specs=(vmem, vmem),
            scratch_shapes=[
                bf16(NB, BLK, 2 * D),
                bf16(NH, NB, SUB, 2 * WIDTH),
                bf16(2, NBLK, BLK, D),
                bf16(NBLK * BLK, D),
                bf16(NBLK * BLK, D),
                *[bf16(NBLK, SUB, w) for w in widths],
                *[bf16(NZ, NB, SUB, w) for w in widths],
                f32(NZ, ROWS, BAND_BLOCKS * BLK),
                f32(NBLK, 8, D),
                f32(NZ, 8, D),
                f32(NZ, 8, D),
                f32(NH, 2, 8, D),
                pltpu.SMEM((NBLK,), jnp.int32),
                dma((4,)), dma, dma((4, NH - 1)), dma((2, NZ)), dma((NZ,)), dma((2, NZ)),
                dma((2, NZ)), dma((NZ,)), dma((NH - 1,)),
                dma, dma((4, NH)), dma((2,)), dma((NZ,)), dma((NZ,)), dma, dma, dma, dma,
            ],
            compiler_params=pltpu.CompilerParams(
                collective_id=0, has_side_effects=True, vmem_limit_bytes=60 << 20
            ),
        )(order, resp, q, k, v)

    rows = P(("dp", "ctx"), "head")
    return jax.shard_map(
        step,
        mesh=mesh,
        in_specs=(rows, rows, rows, P("dp"), P("dp")),
        out_specs=(P(("dp", "ctx"), "head", None), P("head", ("dp", "ctx"))),
        check_vma=False,
    )
```

```python
import functools
import math

import jax
import jax.numpy as jnp
from jax import lax
from jax.experimental import pallas as pl
from jax.experimental.pallas import tpu as pltpu
from jax.sharding import PartitionSpec as P

MESH = pl.DeviceIdType.MESH
D = 128
BLK = 128
NZ = 8
NH = 4
NB = 3
GROUP = 5
SUB = BLK // NH
NBLK = NZ * NB
PROMPT_BLOCKS = 6
BAND_BLOCKS = 8
ROWS = NB * SUB
WIDTH = GROUP * D
CHUNKS = ((0, 3), (3, 5))
SCALE = 1.0 / math.sqrt(D)
LOG2E = 1.4426950408889634
NEG = -1e30
HELD = 5


def kernel(
    order_ref, resp_ref, q_ref, k_ref, v_ref, out_ref, lse_ref,
    vstage, qstage, kv, kseq, vseq, qbuf, obuf, bias,
    lse_seq, lse_send, lse_recv, inv_ref,
    kv_send, v_send, q1_send, q2_send, x_send, c_send, o_send, l_send,
    v_recv, q1_recv, q2_recv, z_recv, x_recv, c_recv, o_recv, l_recv,
):
    z = lax.axis_index("ctx")
    h = lax.axis_index("head")
    x_peer = lax.rem(h + 2, NH)
    c_peer = h + 1 - 2 * lax.rem(h, 2)
    d_peer = lax.rem(c_peer + 2, NH)
    peers = (c_peer, x_peer, d_peer)

    def plane(k):
        return lax.rem(2 * k, NZ) + k // 4

    my_k = z // 2 + 4 * lax.rem(z, 2)
    my_src = my_k // 2

    barrier = pltpu.get_barrier_semaphore()
    for dz in range(1, NZ):
        pl.semaphore_signal(
            barrier, inc=1, device_id={"ctx": lax.rem(z + dz, NZ)}, device_id_type=MESH
        )
    for th in peers:
        pl.semaphore_signal(barrier, inc=1, device_id={"head": th}, device_id_type=MESH)
    for kk in range(2):
        tz = plane(2 * h + kk)

        @pl.when(tz != z)
        def _():
            for th in peers:
                pl.semaphore_signal(
                    barrier, inc=1, device_id={"ctx": tz, "head": th}, device_id_type=MESH
                )

    pl.semaphore_wait(barrier, NZ - 1 + NH - 1 + jnp.where(my_src == h, 0, NZ - 1))

    def remote(src, dst, send_sem, recv_sem, tz, th):
        return pltpu.make_async_remote_copy(
            src, dst, send_sem, recv_sem, device_id={"ctx": tz, "head": th}, device_id_type=MESH
        )

    def send(src, dst, send_sem, recv_sem, tz, th=h):
        mine = (tz == z) & (th == h)

        @pl.when(mine)
        def _():
            pltpu.make_async_copy(src, dst, recv_sem).start()

        @pl.when(jnp.logical_not(mine))
        def _():
            remote(src, dst, send_sem, recv_sem, tz, th).start()

    def sent(src, dst, send_sem, recv_sem, tz, th=h):
        @pl.when(jnp.logical_not((tz == z) & (th == h)))
        def _():
            remote(src, dst, send_sem, recv_sem, tz, th).wait_send()

    def landed(ref, sem):
        pltpu.make_async_copy(ref, ref, sem).wait()

    here = pl.ds(NB * z, NB)

    k_moves = [
        (k_ref.at[:, :, pl.ds(D * kk, D)], kv.at[0, here], kv_send.at[kk], z_recv.at[z],
         plane(2 * h + kk))
        for kk in range(2)
    ]
    v_moves = [
        (vstage.at[:, :, pl.ds(D * kk, D)], kv.at[1, here], kv_send.at[2 + kk], z_recv.at[z],
         plane(2 * x_peer + kk))
        for kk in range(2)
    ]
    v_move = (v_ref, vstage, v_send, v_recv, z, x_peer)
    remote(*v_move).start()
    for move in k_moves:
        send(*move)

    def q_cols(kk):
        return pl.ds(WIDTH * kk, WIDTH)

    def q1_move(e, kk):
        rows = pl.ds(pl.multiple_of(SUB * peers[e], SUB), SUB)
        return (
            q_ref.at[:, rows, q_cols(kk)], qstage.at[h, :, :, q_cols(kk)],
            q1_send.at[kk, e], q1_recv.at[kk, h], z, peers[e],
        )

    q1_moves = [q1_move(e, kk) for e in range(NH - 1) for kk in range(2)]
    for move in q1_moves[:2]:
        remote(*move).start()

    def q2_move(e, hd, kk):
        if e == 0:
            src = q_ref.at[:, pl.ds(pl.multiple_of(SUB * h, SUB), SUB), q_cols(kk)]
        else:
            src = qstage.at[hd, :, :, q_cols(kk)]
        return (src, qbuf.at[here], q2_send.at[e, kk], q2_recv, plane(2 * hd + kk))

    q2_moves = []

    def forward(e):
        hd = (h, *peers)[e]
        for kk in range(2):
            move = q2_move(e, hd, kk)
            if e:
                landed(move[0], q1_recv.at[kk, hd])
            send(*move)
            q2_moves.append(move)

    def find(p, c):
        found = jnp.int32(0)
        for j in range(NBLK):
            found = jnp.where(order_ref[j] == p, j, found)
        inv_ref[p] = found
        return c

    lax.fori_loop(0, NBLK, find, 0)

    lane = lax.broadcasted_iota(jnp.int32, (ROWS, D), 1)
    row = lax.broadcasted_iota(jnp.int32, (ROWS, D), 0)
    row_pos = (row // SUB) * BLK + lax.rem(row, SUB) + SUB * h

    def band_start(o):
        return jnp.where(o < 2, 0, jnp.maximum(PROMPT_BLOCKS, NB * o - 5))

    def masks(o, c):
        q_pos = row_pos + o * (NB * BLK)
        start = jnp.full((ROWS, D), PROMPT_BLOCKS * BLK, jnp.int32)
        end = jnp.int32(PROMPT_BLOCKS * BLK)
        for n in range(resp_ref.shape[0]):
            end = end + resp_ref[n]
            start = jnp.where(q_pos >= end, end, start)
        start = jnp.where(o < 2, 0, start)
        for b in range(BAND_BLOCKS):
            key_pos = lane + (band_start(o) + b) * BLK
            allowed = (key_pos >= start) & (key_pos <= q_pos)
            bias[o, :, pl.ds(b * BLK, BLK)] = jnp.where(allowed, 0.0, NEG)
        return c

    lax.fori_loop(0, NZ, masks, 0)

    landed(vstage, v_recv)
    for move in v_moves:
        send(*move)
    for move in q1_moves[2:]:
        remote(*move).start()
    forward(0)
    forward(1)

    primary = lax.rem(h, 2) == lax.rem(my_src, 2)
    which = lax.rem(h // 2 + my_src // 2, 2)

    def piece(w, s):
        return kv.at[w, pl.ds(NB * s, NB)]

    def x_move(s):
        src = piece(which, s)
        return (src, src, x_send.at[s], x_recv.at[s], z, x_peer)

    def c_move(w, s):
        src = piece(w, s)
        return (src, src, c_send.at[w, s], c_recv, z, c_peer)

    def source(t):
        return lax.rem(z + 4 + ((t + 1) // 2) * (1 - 2 * lax.rem(t, 2)), NZ)

    @pl.when(primary)
    def _():
        def own(t, c):
            s = source(NZ - 1 - t)
            landed(piece(which, s), z_recv.at[s])
            remote(*x_move(s)).start()
            remote(*c_move(which, s)).start()
            return c

        lax.fori_loop(0, NZ, own, 0)

    forward(2)
    forward(3)

    @pl.when(primary)
    def _():
        def other(t, c):
            s = source(NZ - 1 - t)
            landed(piece(1 - which, s), x_recv.at[s])
            remote(*c_move(1 - which, s)).start()
            return c

        lax.fori_loop(0, NZ, other, 0)

    @pl.when(jnp.logical_not(primary))
    def _():
        landed(kv, c_recv)

    def build(p, c):
        j = inv_ref[p]
        at = pl.ds(pl.multiple_of(p * BLK, BLK), BLK)
        kseq[:, at] = kv[0, j].T
        vseq[at, :] = kv[1, j]
        return c

    lax.fori_loop(0, NBLK, build, 0)

    out_col = my_k * WIDTH

    def o_move(c, o):
        first, last = CHUNKS[c]
        size = (last - first) * D
        cols = pl.ds(pl.multiple_of(out_col + first * D, D), size)
        src = obuf.at[o, :, :, pl.ds(first * D, size)]
        return (src, out_ref.at[:, :, cols], o_send.at[c, o], o_recv, o)

    def attend(t, o, spans):
        idx = [inv_ref[NB * o + b] for b in range(NB)]
        tile = jnp.zeros((ROWS, D), jnp.float32)
        for c, (begin, end) in enumerate(CHUNKS):
            n = end - begin
            q = jnp.concatenate(
                [qbuf[j, :, pl.ds(g * D, D)] for g in range(begin, end) for j in idx], axis=0
            )
            scores = []
            for at, use_bias in spans:
                s = jnp.dot(q, kseq[:, at], preferred_element_type=jnp.float32)
                if use_bias:
                    mask = bias[o, :, pl.ds(0, s.shape[1])]
                    s = (s.reshape(n, ROWS, -1) + mask[None]).reshape(s.shape)
                scores.append(s)
            top = functools.reduce(jnp.maximum, [jnp.max(s, axis=1, keepdims=True) for s in scores])
            total = jnp.zeros((n * ROWS, 1), jnp.float32)
            acc = jnp.zeros((n * ROWS, D), jnp.float32)
            for (at, _), s in zip(spans, scores):
                w = jnp.exp2((s - top) * (SCALE * LOG2E))
                total = total + jnp.sum(w, axis=1, keepdims=True)
                acc = acc + jnp.dot(
                    w.astype(jnp.bfloat16), vseq[at, :], preferred_element_type=jnp.float32
                )
            res = (acc / total).astype(jnp.bfloat16)
            lse = top * SCALE + jnp.log(total)
            for i in range(n):
                for b in range(NB):
                    first = i * ROWS + b * SUB
                    obuf[o, b, :, pl.ds((begin + i) * D, D)] = res[first : first + SUB]
                tile = jnp.where(lane == begin + i, lse[i * ROWS : (i + 1) * ROWS], tile)

            @pl.when(t < HELD)
            def _():
                send(*o_move(c, o))

        tile = jnp.concatenate([tile, jnp.zeros((D - ROWS, D), jnp.float32)], axis=0).T[:8]
        for b in range(NB):
            lse_seq[NB * o + b] = tile if b == 0 else pltpu.roll(tile, D - SUB * b, 1)

    landed(qbuf, q2_recv)

    def owner(t, carry):
        o = source(t)

        @pl.when(o < 2)
        def _():
            attend(t, o, [(pl.ds(0, PROMPT_BLOCKS * BLK), True)])

        @pl.when(o >= 2)
        def _():
            first = pl.multiple_of(band_start(o) * BLK, BLK)
            attend(t, o, [
                (pl.ds(0, PROMPT_BLOCKS * BLK), False),
                (pl.ds(first, BAND_BLOCKS * BLK), True),
            ])

        return carry

    lax.fori_loop(0, NZ, owner, 0)

    lane8 = lax.broadcasted_iota(jnp.int32, (8, D), 1)

    def l_move(s):
        return (lse_send.at[s], lse_recv.at[h, lax.rem(my_k, 2)], l_send.at[s], l_recv, s, my_src)

    for s in range(NZ):
        tile = lse_seq[order_ref[NB * s]]
        for b in range(1, NB):
            tile = jnp.where(
                lane8 >= SUB * b, pltpu.roll(lse_seq[order_ref[NB * s + b]], SUB * b, 1), tile
            )
        lse_send[s] = tile
        send(*l_move(s))

    def rest(t, carry):
        for c in range(len(CHUNKS)):
            send(*o_move(c, source(t)))
        return carry

    lax.fori_loop(HELD, NZ, rest, 0)
    landed(lse_recv, l_recv)
    for kk in range(2):
        for b in range(NB):
            tile = jnp.zeros((8, D), jnp.float32)
            for r in range(NH):
                shift = (SUB * (r - b)) % D
                part = lse_recv[r, kk]
                part = pltpu.roll(part, shift, 1) if shift else part
                tile = jnp.where(lane8 >= SUB * r, part, tile)
            lse_ref[pl.ds(kk * GROUP, GROUP), pl.ds(b * BLK, BLK)] = tile[:GROUP]

    remote(*v_move).wait_send()
    for move in k_moves + v_moves + q2_moves:
        sent(*move)
    for move in q1_moves:
        remote(*move).wait_send()

    @pl.when(primary)
    def _():
        def done(s, c):
            remote(*x_move(s)).wait_send()
            remote(*c_move(0, s)).wait_send()
            remote(*c_move(1, s)).wait_send()
            return c

        lax.fori_loop(0, NZ, done, 0)

    for s in range(NZ):
        sent(*l_move(jnp.int32(s)))
        for c in range(2):
            sent(*o_move(c, jnp.int32(s)))
    landed(out_ref, o_recv)


def solution(mesh):
    def step(q, k, v, order, resp):
        q = q.reshape(NB, BLK, q.shape[1])
        k = k.reshape(NB, BLK, k.shape[1])
        v = v.reshape(NB, BLK, v.shape[1])
        smem = pl.BlockSpec(memory_space=pltpu.SMEM)
        hbm = pl.BlockSpec(memory_space=pl.ANY)
        vmem = pl.BlockSpec(memory_space=pltpu.VMEM)
        dma = pltpu.SemaphoreType.DMA
        bf16 = lambda *shape: pltpu.VMEM(shape, jnp.bfloat16)
        f32 = lambda *shape: pltpu.VMEM(shape, jnp.float32)
        return pl.pallas_call(
            kernel,
            out_shape=(
                jax.ShapeDtypeStruct((NB, SUB, NZ * WIDTH), jnp.bfloat16),
                jax.ShapeDtypeStruct((2 * GROUP, NB * BLK), jnp.float32),
            ),
            in_specs=[smem, smem, hbm, hbm, hbm],
            out_specs=(hbm, vmem),
            scratch_shapes=[
                bf16(NB, BLK, 2 * D),
                bf16(NH, NB, SUB, 2 * WIDTH),
                bf16(2, NBLK, BLK, D),
                bf16(D, NBLK * BLK),
                bf16(NBLK * BLK, D),
                bf16(NBLK, SUB, WIDTH),
                bf16(NZ, NB, SUB, WIDTH),
                f32(NZ, ROWS, BAND_BLOCKS * BLK),
                f32(NBLK, 8, D),
                f32(NZ, 8, D),
                f32(NH, 2, 8, D),
                pltpu.SMEM((NBLK,), jnp.int32),
                dma((4,)), dma, dma((2, NH - 1)), dma((NH, 2)), dma((NZ,)), dma((2, NZ)),
                dma((2, NZ)), dma((NZ,)),
                dma, dma((2, NH)), dma, dma((NZ,)), dma((NZ,)), dma, dma, dma,
            ],
            compiler_params=pltpu.CompilerParams(
                collective_id=0, has_side_effects=True, vmem_limit_bytes=60 << 20
            ),
        )(order, resp, q, k, v)

    rows = P(("dp", "ctx"), "head")
    return jax.shard_map(
        step,
        mesh=mesh,
        in_specs=(rows, rows, rows, P("dp"), P("dp")),
        out_specs=(P(("dp", "ctx"), "head", None), P("head", ("dp", "ctx"))),
        check_vma=False,
    )
```

```python
import functools
import math

import jax
import jax.numpy as jnp
from jax import lax
from jax.experimental import pallas as pl
from jax.experimental.pallas import tpu as pltpu
from jax.sharding import PartitionSpec as P

MESH = pl.DeviceIdType.MESH
D = 128
BLK = 128
NZ = 8
NH = 4
NB = 3
GROUP = 5
SUB = BLK // NH
NBLK = NZ * NB
PROMPT_BLOCKS = 6
BAND_BLOCKS = 8
ROWS = NB * SUB
WIDTH = GROUP * D
CHUNKS = ((0, 3), (3, 5))
SCALE = 1.0 / math.sqrt(D)
LOG2E = 1.4426950408889634
NEG = -1e30


def kernel(
    order_ref, resp_ref, q_ref, k_ref, v_ref, out_ref, lse_ref,
    vstage, qstage, kv, kseq, vseq, qbuf_a, qbuf_b, obuf, bias,
    lse_seq, lse_send, lse_recv, inv_ref,
    kv_send, v_send, q1_send, q2_send, x_send, c_send, o_send, l_send,
    v_recv, q1_recv, q2_recv, z_recv, x_recv, c_recv, o_recv, l_recv,
):
    z = lax.axis_index("ctx")
    h = lax.axis_index("head")
    x_peer = lax.rem(h + 2, NH)
    c_peer = h + 1 - 2 * lax.rem(h, 2)
    d_peer = lax.rem(c_peer + 2, NH)
    peers = (c_peer, x_peer, d_peer)
    qbuf = (qbuf_a, qbuf_b)

    def plane(k):
        return lax.rem(2 * k, NZ) + k // 4

    my_k = z // 2 + 4 * lax.rem(z, 2)
    my_src = my_k // 2

    barrier = pltpu.get_barrier_semaphore()
    for dz in range(1, NZ):
        pl.semaphore_signal(
            barrier, inc=1, device_id={"ctx": lax.rem(z + dz, NZ)}, device_id_type=MESH
        )
    for th in peers:
        pl.semaphore_signal(barrier, inc=1, device_id={"head": th}, device_id_type=MESH)
    for kk in range(2):
        tz = plane(2 * h + kk)

        @pl.when(tz != z)
        def _():
            for th in peers:
                pl.semaphore_signal(
                    barrier, inc=1, device_id={"ctx": tz, "head": th}, device_id_type=MESH
                )

    pl.semaphore_wait(barrier, NZ - 1 + NH - 1 + jnp.where(my_src == h, 0, NZ - 1))

    def remote(src, dst, send_sem, recv_sem, tz, th):
        return pltpu.make_async_remote_copy(
            src, dst, send_sem, recv_sem, device_id={"ctx": tz, "head": th}, device_id_type=MESH
        )

    def send(src, dst, send_sem, recv_sem, tz, th=h):
        mine = (tz == z) & (th == h)

        @pl.when(mine)
        def _():
            pltpu.make_async_copy(src, dst, recv_sem).start()

        @pl.when(jnp.logical_not(mine))
        def _():
            remote(src, dst, send_sem, recv_sem, tz, th).start()

    def sent(src, dst, send_sem, recv_sem, tz, th=h):
        @pl.when(jnp.logical_not((tz == z) & (th == h)))
        def _():
            remote(src, dst, send_sem, recv_sem, tz, th).wait_send()

    def landed(ref, sem):
        pltpu.make_async_copy(ref, ref, sem).wait()

    here = pl.ds(NB * z, NB)

    k_moves = [
        (k_ref.at[:, :, pl.ds(D * kk, D)], kv.at[0, here], kv_send.at[kk], z_recv.at[z],
         plane(2 * h + kk))
        for kk in range(2)
    ]
    v_moves = [
        (vstage.at[:, :, pl.ds(D * kk, D)], kv.at[1, here], kv_send.at[2 + kk], z_recv.at[z],
         plane(2 * x_peer + kk))
        for kk in range(2)
    ]
    v1_moves = [
        (v_ref.at[:, :, pl.ds(D * kk, D)], vstage.at[:, :, pl.ds(D * kk, D)],
         v_send.at[kk], v_recv.at[kk], z, x_peer)
        for kk in range(2)
    ]
    for move in v1_moves:
        remote(*move).start()
    for move in k_moves:
        send(*move)

    def q_cols(c, kk):
        first, last = CHUNKS[c]
        return pl.ds(WIDTH * kk + D * first, D * (last - first))

    def q1_move(c, kk, e):
        rows = pl.ds(pl.multiple_of(SUB * peers[e], SUB), SUB)
        n = 2 * c + kk
        return (
            q_ref.at[:, rows, q_cols(c, kk)], qstage.at[h, :, :, q_cols(c, kk)],
            q1_send.at[n, e], q1_recv.at[n, h], z, peers[e],
        )

    q1_moves = [q1_move(c, kk, e) for c in range(2) for kk in range(2) for e in range(NH - 1)]

    def share_queries(c, *where):
        for e in where:
            for kk in range(2):
                remote(*q1_move(c, kk, e)).start()

    def q2_move(c, e, kk):
        hd = (h, *peers)[e]
        if e == 0:
            src = q_ref.at[:, pl.ds(pl.multiple_of(SUB * h, SUB), SUB), q_cols(c, kk)]
        else:
            src = qstage.at[hd, :, :, q_cols(c, kk)]
        return (
            src, qbuf[c].at[here], q2_send.at[c, 2 * e + kk], q2_recv.at[c], plane(2 * hd + kk),
        )

    q2_moves = [q2_move(c, e, kk) for c in range(2) for e in range(NH) for kk in range(2)]

    def forward(c, e):
        for kk in range(2):
            move = q2_move(c, e, kk)
            if e:
                landed(move[0], q1_recv.at[2 * c + kk, (h, *peers)[e]])
            send(*move)

    share_queries(0, 0)
    share_queries(1, 0)

    def find(p, c):
        found = jnp.int32(0)
        for j in range(NBLK):
            found = jnp.where(order_ref[j] == p, j, found)
        inv_ref[p] = found
        return c

    lax.fori_loop(0, NBLK, find, 0)

    lane = lax.broadcasted_iota(jnp.int32, (ROWS, D), 1)
    row = lax.broadcasted_iota(jnp.int32, (ROWS, D), 0)
    row_pos = (row // SUB) * BLK + lax.rem(row, SUB) + SUB * h

    def band_start(o):
        return jnp.where(o < 2, 0, jnp.maximum(PROMPT_BLOCKS, NB * o - 5))

    def masks(o, c):
        q_pos = row_pos + o * (NB * BLK)
        start = jnp.full((ROWS, D), PROMPT_BLOCKS * BLK, jnp.int32)
        end = jnp.int32(PROMPT_BLOCKS * BLK)
        for n in range(resp_ref.shape[0]):
            end = end + resp_ref[n]
            start = jnp.where(q_pos >= end, end, start)
        start = jnp.where(o < 2, 0, start)
        for b in range(BAND_BLOCKS):
            key_pos = lane + (band_start(o) + b) * BLK
            allowed = (key_pos >= start) & (key_pos <= q_pos)
            bias[o, :, pl.ds(b * BLK, BLK)] = jnp.where(allowed, 0.0, NEG)
        return c

    lax.fori_loop(0, NZ, masks, 0)

    for kk in range(2):
        landed(v_moves[kk][0], v_recv.at[kk])
        send(*v_moves[kk])
    share_queries(0, 1, 2)
    forward(0, 0)
    forward(0, 1)

    primary = lax.rem(h, 2) == lax.rem(my_src, 2)
    which = lax.rem(h // 2 + my_src // 2, 2)

    def piece(w, s):
        return kv.at[w, pl.ds(NB * s, NB)]

    def x_move(s):
        src = piece(which, s)
        return (src, src, x_send.at[s], x_recv.at[s], z, x_peer)

    def c_move(w, s):
        src = piece(w, s)
        return (src, src, c_send.at[w, s], c_recv, z, c_peer)

    def source(t):
        return lax.rem(z + 4 + ((t + 1) // 2) * (1 - 2 * lax.rem(t, 2)), NZ)

    @pl.when(primary)
    def _():
        def own(t, c):
            s = source(NZ - 1 - t)
            landed(piece(which, s), z_recv.at[s])
            remote(*x_move(s)).start()
            remote(*c_move(which, s)).start()
            return c

        lax.fori_loop(0, NZ, own, 0)

    forward(0, 2)
    forward(0, 3)
    share_queries(1, 1, 2)
    forward(1, 0)
    forward(1, 1)

    @pl.when(primary)
    def _():
        def other(t, c):
            s = source(NZ - 1 - t)
            landed(piece(1 - which, s), x_recv.at[s])
            remote(*c_move(1 - which, s)).start()
            return c

        lax.fori_loop(0, NZ, other, 0)

    forward(1, 2)
    forward(1, 3)

    @pl.when(jnp.logical_not(primary))
    def _():
        landed(kv, c_recv)

    def build(p, c):
        j = inv_ref[p]
        at = pl.ds(pl.multiple_of(p * BLK, BLK), BLK)
        kseq[:, at] = kv[0, j].T
        vseq[at, :] = kv[1, j]
        return c

    lax.fori_loop(0, NBLK, build, 0)

    out_col = my_k * WIDTH

    def o_move(c, o):
        first, last = CHUNKS[c]
        size = (last - first) * D
        cols = pl.ds(pl.multiple_of(out_col + first * D, D), size)
        src = obuf.at[o, :, :, pl.ds(first * D, size)]
        return (src, out_ref.at[:, :, cols], o_send.at[c, o], o_recv, o)

    def attend(c, o, spans):
        idx = [inv_ref[NB * o + b] for b in range(NB)]
        begin, end = CHUNKS[c]
        n = end - begin
        q = jnp.concatenate(
            [qbuf[c][j, :, pl.ds(g * D, D)] for g in range(n) for j in idx], axis=0
        )
        scores = []
        for at, use_bias in spans:
            s = jnp.dot(q, kseq[:, at], preferred_element_type=jnp.float32)
            if use_bias:
                mask = bias[o, :, pl.ds(0, s.shape[1])]
                s = (s.reshape(n, ROWS, -1) + mask[None]).reshape(s.shape)
            scores.append(s)
        top = functools.reduce(jnp.maximum, [jnp.max(s, axis=1, keepdims=True) for s in scores])
        total = jnp.zeros((n * ROWS, 1), jnp.float32)
        acc = jnp.zeros((n * ROWS, D), jnp.float32)
        for (at, _), s in zip(spans, scores):
            w = jnp.exp2((s - top) * (SCALE * LOG2E))
            total = total + jnp.sum(w, axis=1, keepdims=True)
            acc = acc + jnp.dot(
                w.astype(jnp.bfloat16), vseq[at, :], preferred_element_type=jnp.float32
            )
        res = (acc / total).astype(jnp.bfloat16)
        lse = top * SCALE + jnp.log(total)
        tile = jnp.zeros((ROWS, D), jnp.float32)
        for i in range(n):
            for b in range(NB):
                first = i * ROWS + b * SUB
                obuf[o, b, :, pl.ds((begin + i) * D, D)] = res[first : first + SUB]
            tile = jnp.where(lane == begin + i, lse[i * ROWS : (i + 1) * ROWS], tile)
        tile = jnp.concatenate([tile, jnp.zeros((D - ROWS, D), jnp.float32)], axis=0).T[:8]
        for b in range(NB):
            part = tile if b == 0 else pltpu.roll(tile, D - SUB * b, 1)
            lse_seq[NB * o + b] = part if c == 0 else part + lse_seq[NB * o + b]

    for c in range(2):
        landed(qbuf[c], q2_recv.at[c])

        def owner(t, carry, c=c):
            o = source(t)

            @pl.when(o < 2)
            def _():
                attend(c, o, [(pl.ds(0, PROMPT_BLOCKS * BLK), True)])

            @pl.when(o >= 2)
            def _():
                first = pl.multiple_of(band_start(o) * BLK, BLK)
                attend(c, o, [
                    (pl.ds(0, PROMPT_BLOCKS * BLK), False),
                    (pl.ds(first, BAND_BLOCKS * BLK), True),
                ])

            send(*o_move(c, o))
            return carry

        lax.fori_loop(0, NZ, owner, 0)

    lane8 = lax.broadcasted_iota(jnp.int32, (8, D), 1)

    def l_move(s):
        return (lse_send.at[s], lse_recv.at[h, lax.rem(my_k, 2)], l_send.at[s], l_recv, s, my_src)

    for s in range(NZ):
        tile = lse_seq[order_ref[NB * s]]
        for b in range(1, NB):
            tile = jnp.where(
                lane8 >= SUB * b, pltpu.roll(lse_seq[order_ref[NB * s + b]], SUB * b, 1), tile
            )
        lse_send[s] = tile
        send(*l_move(s))

    landed(lse_recv, l_recv)
    for kk in range(2):
        for b in range(NB):
            tile = jnp.zeros((8, D), jnp.float32)
            for r in range(NH):
                shift = (SUB * (r - b)) % D
                part = lse_recv[r, kk]
                part = pltpu.roll(part, shift, 1) if shift else part
                tile = jnp.where(lane8 >= SUB * r, part, tile)
            lse_ref[pl.ds(kk * GROUP, GROUP), pl.ds(b * BLK, BLK)] = tile[:GROUP]

    for move in v1_moves:
        remote(*move).wait_send()
    for move in k_moves + v_moves + q2_moves:
        sent(*move)
    for move in q1_moves:
        remote(*move).wait_send()

    @pl.when(primary)
    def _():
        def done(s, c):
            remote(*x_move(s)).wait_send()
            remote(*c_move(0, s)).wait_send()
            remote(*c_move(1, s)).wait_send()
            return c

        lax.fori_loop(0, NZ, done, 0)

    for s in range(NZ):
        sent(*l_move(jnp.int32(s)))
        for c in range(2):
            sent(*o_move(c, jnp.int32(s)))
    landed(out_ref, o_recv)


def solution(mesh):
    def step(q, k, v, order, resp):
        q = q.reshape(NB, BLK, q.shape[1])
        k = k.reshape(NB, BLK, k.shape[1])
        v = v.reshape(NB, BLK, v.shape[1])
        smem = pl.BlockSpec(memory_space=pltpu.SMEM)
        hbm = pl.BlockSpec(memory_space=pl.ANY)
        vmem = pl.BlockSpec(memory_space=pltpu.VMEM)
        dma = pltpu.SemaphoreType.DMA
        bf16 = lambda *shape: pltpu.VMEM(shape, jnp.bfloat16)
        f32 = lambda *shape: pltpu.VMEM(shape, jnp.float32)
        return pl.pallas_call(
            kernel,
            out_shape=(
                jax.ShapeDtypeStruct((NB, SUB, NZ * WIDTH), jnp.bfloat16),
                jax.ShapeDtypeStruct((2 * GROUP, NB * BLK), jnp.float32),
            ),
            in_specs=[smem, smem, hbm, hbm, hbm],
            out_specs=(hbm, vmem),
            scratch_shapes=[
                bf16(NB, BLK, 2 * D),
                bf16(NH, NB, SUB, 2 * WIDTH),
                bf16(2, NBLK, BLK, D),
                bf16(D, NBLK * BLK),
                bf16(NBLK * BLK, D),
                *[bf16(NBLK, SUB, D * (last - first)) for first, last in CHUNKS],
                bf16(NZ, NB, SUB, WIDTH),
                f32(NZ, ROWS, BAND_BLOCKS * BLK),
                f32(NBLK, 8, D),
                f32(NZ, 8, D),
                f32(NH, 2, 8, D),
                pltpu.SMEM((NBLK,), jnp.int32),
                dma((4,)), dma((2,)), dma((4, NH - 1)), dma((2, NZ)), dma((NZ,)), dma((2, NZ)),
                dma((2, NZ)), dma((NZ,)),
                dma((2,)), dma((4, NH)), dma((2,)), dma((NZ,)), dma((NZ,)), dma, dma, dma,
            ],
            compiler_params=pltpu.CompilerParams(
                collective_id=0, has_side_effects=True, vmem_limit_bytes=60 << 20
            ),
        )(order, resp, q, k, v)

    rows = P(("dp", "ctx"), "head")
    return jax.shard_map(
        step,
        mesh=mesh,
        in_specs=(rows, rows, rows, P("dp"), P("dp")),
        out_specs=(P(("dp", "ctx"), "head", None), P("head", ("dp", "ctx"))),
        check_vma=False,
    )
```

```python
import functools
import math

import jax
import jax.numpy as jnp
from jax import lax
from jax.experimental import pallas as pl
from jax.experimental.pallas import tpu as pltpu
from jax.sharding import PartitionSpec as P

MESH = pl.DeviceIdType.MESH
D = 128
BLK = 128
NZ = 8
NH = 4
NB = 3
GROUP = 5
SUB = BLK // NH
NBLK = NZ * NB
PROMPT_BLOCKS = 6
BAND_BLOCKS = 8
ROWS = NB * SUB
WIDTH = GROUP * D
CHUNKS = ((0, 3), (3, 5))
SCALE = 1.0 / math.sqrt(D)
LOG2E = 1.4426950408889634
NEG = -1e30


def kernel(
    order_ref, resp_ref, q_ref, k_ref, v_ref, out_ref, lse_ref,
    vstage, qstage, kv, kseq, vseq, qbuf_a, qbuf_b, obuf, bias,
    lse_seq, lse_send, lse_recv, inv_ref,
    kv_send, v_send, q1_send, q2_send, x_send, c_send, o_send, l_send,
    v_recv, q1_recv, q2_recv, z_recv, x_recv, c_recv, o_recv, l_recv,
):
    z = lax.axis_index("ctx")
    h = lax.axis_index("head")
    x_peer = lax.rem(h + 2, NH)
    c_peer = h + 1 - 2 * lax.rem(h, 2)
    d_peer = lax.rem(c_peer + 2, NH)
    peers = (c_peer, x_peer, d_peer)
    qbuf = (qbuf_a, qbuf_b)

    def plane(k):
        return lax.rem(2 * k, NZ) + k // 4

    my_k = z // 2 + 4 * lax.rem(z, 2)
    my_src = my_k // 2

    barrier = pltpu.get_barrier_semaphore()
    for dz in range(1, NZ):
        pl.semaphore_signal(
            barrier, inc=1, device_id={"ctx": lax.rem(z + dz, NZ)}, device_id_type=MESH
        )
    for th in peers:
        pl.semaphore_signal(barrier, inc=1, device_id={"head": th}, device_id_type=MESH)
    for kk in range(2):
        tz = plane(2 * h + kk)

        @pl.when(tz != z)
        def _():
            for th in peers:
                pl.semaphore_signal(
                    barrier, inc=1, device_id={"ctx": tz, "head": th}, device_id_type=MESH
                )

    pl.semaphore_wait(barrier, NZ - 1 + NH - 1 + jnp.where(my_src == h, 0, NZ - 1))

    def remote(src, dst, send_sem, recv_sem, tz, th):
        return pltpu.make_async_remote_copy(
            src, dst, send_sem, recv_sem, device_id={"ctx": tz, "head": th}, device_id_type=MESH
        )

    def send(src, dst, send_sem, recv_sem, tz, th=h):
        mine = (tz == z) & (th == h)

        @pl.when(mine)
        def _():
            pltpu.make_async_copy(src, dst, recv_sem).start()

        @pl.when(jnp.logical_not(mine))
        def _():
            remote(src, dst, send_sem, recv_sem, tz, th).start()

    def sent(src, dst, send_sem, recv_sem, tz, th=h):
        @pl.when(jnp.logical_not((tz == z) & (th == h)))
        def _():
            remote(src, dst, send_sem, recv_sem, tz, th).wait_send()

    def landed(ref, sem):
        pltpu.make_async_copy(ref, ref, sem).wait()

    here = pl.ds(NB * z, NB)

    k_moves = [
        (k_ref.at[:, :, pl.ds(D * kk, D)], kv.at[0, here], kv_send.at[kk], z_recv.at[z],
         plane(2 * h + kk))
        for kk in range(2)
    ]
    v_moves = [
        (vstage.at[:, :, pl.ds(D * kk, D)], kv.at[1, here], kv_send.at[2 + kk], z_recv.at[z],
         plane(2 * x_peer + kk))
        for kk in range(2)
    ]
    v1_moves = [
        (v_ref.at[:, :, pl.ds(D * kk, D)], vstage.at[:, :, pl.ds(D * kk, D)],
         v_send.at[kk], v_recv.at[kk], z, x_peer)
        for kk in range(2)
    ]
    for move in v1_moves:
        remote(*move).start()
    for move in k_moves:
        send(*move)

    def q_cols(c, kk):
        first, last = CHUNKS[c]
        return pl.ds(WIDTH * kk + D * first, D * (last - first))

    def q1_move(c, kk, e):
        rows = pl.ds(pl.multiple_of(SUB * peers[e], SUB), SUB)
        n = 2 * c + kk
        return (
            q_ref.at[:, rows, q_cols(c, kk)], qstage.at[h, :, :, q_cols(c, kk)],
            q1_send.at[n, e], q1_recv.at[n, h], z, peers[e],
        )

    q1_moves = [q1_move(c, kk, e) for c in range(2) for kk in range(2) for e in range(NH - 1)]

    def share_queries(c, *where):
        for e in where:
            for kk in range(2):
                remote(*q1_move(c, kk, e)).start()

    def q2_move(c, e, kk):
        hd = (h, *peers)[e]
        if e == 0:
            src = q_ref.at[:, pl.ds(pl.multiple_of(SUB * h, SUB), SUB), q_cols(c, kk)]
        else:
            src = qstage.at[hd, :, :, q_cols(c, kk)]
        return (
            src, qbuf[c].at[here], q2_send.at[c, 2 * e + kk], q2_recv.at[c], plane(2 * hd + kk),
        )

    q2_moves = [q2_move(c, e, kk) for c in range(2) for e in range(NH) for kk in range(2)]

    def forward(c, e):
        for kk in range(2):
            move = q2_move(c, e, kk)
            if e:
                landed(move[0], q1_recv.at[2 * c + kk, (h, *peers)[e]])
            send(*move)

    share_queries(0, 0)
    share_queries(1, 0)

    def find(p, c):
        found = jnp.int32(0)
        for j in range(NBLK):
            found = jnp.where(order_ref[j] == p, j, found)
        inv_ref[p] = found
        return c

    lax.fori_loop(0, NBLK, find, 0)

    lane = lax.broadcasted_iota(jnp.int32, (ROWS, D), 1)
    row = lax.broadcasted_iota(jnp.int32, (ROWS, D), 0)
    row_pos = (row // SUB) * BLK + lax.rem(row, SUB) + SUB * h

    def band_start(o):
        return jnp.where(o < 2, 0, jnp.maximum(PROMPT_BLOCKS, NB * o - 5))

    def masks(o, c):
        q_pos = row_pos + o * (NB * BLK)
        start = jnp.full((ROWS, D), PROMPT_BLOCKS * BLK, jnp.int32)
        end = jnp.int32(PROMPT_BLOCKS * BLK)
        for n in range(resp_ref.shape[0]):
            end = end + resp_ref[n]
            start = jnp.where(q_pos >= end, end, start)
        start = jnp.where(o < 2, 0, start)
        for b in range(BAND_BLOCKS):
            key_pos = lane + (band_start(o) + b) * BLK
            allowed = (key_pos >= start) & (key_pos <= q_pos)
            bias[o, :, pl.ds(b * BLK, BLK)] = jnp.where(allowed, 0.0, NEG)
        return c

    lax.fori_loop(0, NZ, masks, 0)

    for kk in range(2):
        landed(v_moves[kk][0], v_recv.at[kk])
        send(*v_moves[kk])
    share_queries(0, 1, 2)
    forward(0, 0)
    forward(0, 1)

    primary = lax.rem(h, 2) == lax.rem(my_src, 2)
    which = lax.rem(h // 2 + my_src // 2, 2)

    def piece(w, s):
        return kv.at[w, pl.ds(NB * s, NB)]

    def x_move(s):
        src = piece(which, s)
        return (src, src, x_send.at[s], x_recv.at[s], z, x_peer)

    def c_move(w, s):
        src = piece(w, s)
        return (src, src, c_send.at[w, s], c_recv, z, c_peer)

    def source(t):
        return lax.rem(z + 4 + ((t + 1) // 2) * (1 - 2 * lax.rem(t, 2)), NZ)

    @pl.when(primary)
    def _():
        def own(t, c):
            s = source(NZ - 1 - t)
            landed(piece(which, s), z_recv.at[s])
            remote(*x_move(s)).start()
            remote(*c_move(which, s)).start()
            return c

        lax.fori_loop(0, NZ, own, 0)

    forward(0, 2)
    forward(0, 3)
    share_queries(1, 1, 2)
    forward(1, 0)
    forward(1, 1)

    @pl.when(primary)
    def _():
        def other(t, c):
            s = source(NZ - 1 - t)
            landed(piece(1 - which, s), x_recv.at[s])
            remote(*c_move(1 - which, s)).start()
            return c

        lax.fori_loop(0, NZ, other, 0)

    forward(1, 2)
    forward(1, 3)

    @pl.when(jnp.logical_not(primary))
    def _():
        landed(kv, c_recv)

    def build(p, c):
        j = inv_ref[p]
        at = pl.ds(pl.multiple_of(p * BLK, BLK), BLK)
        kseq[:, at] = kv[0, j].T
        vseq[at, :] = kv[1, j]
        return c

    lax.fori_loop(0, NBLK, build, 0)

    out_col = my_k * WIDTH

    def o_move(c, o):
        first, last = CHUNKS[c]
        size = (last - first) * D
        cols = pl.ds(pl.multiple_of(out_col + first * D, D), size)
        src = obuf.at[o, :, :, pl.ds(first * D, size)]
        return (src, out_ref.at[:, :, cols], o_send.at[c, o], o_recv, o)

    def attend(c, o, spans):
        idx = [inv_ref[NB * o + b] for b in range(NB)]
        begin, end = CHUNKS[c]
        n = end - begin
        q = jnp.concatenate(
            [qbuf[c][j, :, pl.ds(g * D, D)] for g in range(n) for j in idx], axis=0
        )
        scores = []
        for at, use_bias in spans:
            s = jnp.dot(q, kseq[:, at], preferred_element_type=jnp.float32)
            if use_bias:
                mask = bias[o, :, pl.ds(0, s.shape[1])]
                s = (s.reshape(n, ROWS, -1) + mask[None]).reshape(s.shape)
            scores.append(s)
        top = functools.reduce(jnp.maximum, [jnp.max(s, axis=1, keepdims=True) for s in scores])
        total = jnp.zeros((n * ROWS, 1), jnp.float32)
        acc = jnp.zeros((n * ROWS, D), jnp.float32)
        for (at, _), s in zip(spans, scores):
            w = jnp.exp2((s - top) * (SCALE * LOG2E))
            total = total + jnp.sum(w, axis=1, keepdims=True)
            acc = acc + jnp.dot(
                w.astype(jnp.bfloat16), vseq[at, :], preferred_element_type=jnp.float32
            )
        res = (acc / total).astype(jnp.bfloat16)
        lse = top * SCALE + jnp.log(total)
        tile = jnp.zeros((ROWS, D), jnp.float32)
        for i in range(n):
            for b in range(NB):
                first = i * ROWS + b * SUB
                obuf[o, b, :, pl.ds((begin + i) * D, D)] = res[first : first + SUB]
            tile = jnp.where(lane == begin + i, lse[i * ROWS : (i + 1) * ROWS], tile)
        tile = jnp.concatenate([tile, jnp.zeros((D - ROWS, D), jnp.float32)], axis=0).T[:8]
        for b in range(NB):
            part = tile if b == 0 else pltpu.roll(tile, D - SUB * b, 1)
            lse_seq[NB * o + b] = part if c == 0 else part + lse_seq[NB * o + b]

    for c in range(2):
        landed(qbuf[c], q2_recv.at[c])

        def owner(t, carry, c=c):
            o = source(t)

            @pl.when(o < 2)
            def _():
                attend(c, o, [(pl.ds(0, PROMPT_BLOCKS * BLK), True)])

            @pl.when(o >= 2)
            def _():
                first = pl.multiple_of(band_start(o) * BLK, BLK)
                attend(c, o, [
                    (pl.ds(0, PROMPT_BLOCKS * BLK), False),
                    (pl.ds(first, BAND_BLOCKS * BLK), True),
                ])

            send(*o_move(c, o))
            return carry

        lax.fori_loop(0, NZ, owner, 0)

    lane8 = lax.broadcasted_iota(jnp.int32, (8, D), 1)

    def l_move(s):
        return (lse_send.at[s], lse_recv.at[h, lax.rem(my_k, 2)], l_send.at[s], l_recv, s, my_src)

    for s in range(NZ):
        tile = lse_seq[order_ref[NB * s]]
        for b in range(1, NB):
            tile = jnp.where(
                lane8 >= SUB * b, pltpu.roll(lse_seq[order_ref[NB * s + b]], SUB * b, 1), tile
            )
        lse_send[s] = tile
        send(*l_move(s))

    landed(lse_recv, l_recv)
    for kk in range(2):
        for b in range(NB):
            tile = jnp.zeros((8, D), jnp.float32)
            for r in range(NH):
                shift = (SUB * (r - b)) % D
                part = lse_recv[r, kk]
                part = pltpu.roll(part, shift, 1) if shift else part
                tile = jnp.where(lane8 >= SUB * r, part, tile)
            lse_ref[pl.ds(kk * GROUP, GROUP), pl.ds(b * BLK, BLK)] = tile[:GROUP]

    for move in v1_moves:
        remote(*move).wait_send()
    for move in k_moves + v_moves + q2_moves:
        sent(*move)
    for move in q1_moves:
        remote(*move).wait_send()

    @pl.when(primary)
    def _():
        def done(s, c):
            remote(*x_move(s)).wait_send()
            remote(*c_move(0, s)).wait_send()
            remote(*c_move(1, s)).wait_send()
            return c

        lax.fori_loop(0, NZ, done, 0)

    for s in range(NZ):
        sent(*l_move(jnp.int32(s)))
        for c in range(2):
            sent(*o_move(c, jnp.int32(s)))
    landed(out_ref, o_recv)


def finish(out_ref, lse_ref, out, lse, out_v, lse_v, sem, sem2):
    pairs = [(out_ref.at[b], out_v.at[b], out.at[b]) for b in range(NB)] + [(lse_ref, lse_v, lse)]
    ins = [pltpu.make_async_copy(p[0], p[1], sem.at[i]) for i, p in enumerate(pairs)]
    outs = [pltpu.make_async_copy(p[1], p[2], sem2.at[i]) for i, p in enumerate(pairs)]
    for copy in ins:
        copy.start()
    for i, o in zip(ins, outs):
        i.wait()
        o.start()
    for o in outs:
        o.wait()


def solution(mesh):
    def step(q, k, v, order, resp):
        q = q.reshape(NB, BLK, q.shape[1])
        k = k.reshape(NB, BLK, k.shape[1])
        v = v.reshape(NB, BLK, v.shape[1])
        smem = pl.BlockSpec(memory_space=pltpu.SMEM)
        hbm = pl.BlockSpec(memory_space=pl.ANY)
        vmem = pl.BlockSpec(memory_space=pltpu.VMEM)
        dma = pltpu.SemaphoreType.DMA
        bf16 = lambda *shape: pltpu.VMEM(shape, jnp.bfloat16)
        f32 = lambda *shape: pltpu.VMEM(shape, jnp.float32)
        out, lse = pl.pallas_call(
            kernel,
            out_shape=(
                jax.ShapeDtypeStruct((NB, SUB, NZ * WIDTH), jnp.bfloat16),
                jax.ShapeDtypeStruct((2 * GROUP, NB * BLK), jnp.float32),
            ),
            in_specs=[smem, smem, hbm, hbm, hbm],
            out_specs=(hbm, vmem),
            scratch_shapes=[
                bf16(NB, BLK, 2 * D),
                bf16(NH, NB, SUB, 2 * WIDTH),
                bf16(2, NBLK, BLK, D),
                bf16(D, NBLK * BLK),
                bf16(NBLK * BLK, D),
                *[bf16(NBLK, SUB, D * (last - first)) for first, last in CHUNKS],
                bf16(NZ, NB, SUB, WIDTH),
                f32(NZ, ROWS, BAND_BLOCKS * BLK),
                f32(NBLK, 8, D),
                f32(NZ, 8, D),
                f32(NH, 2, 8, D),
                pltpu.SMEM((NBLK,), jnp.int32),
                dma((4,)), dma((2,)), dma((4, NH - 1)), dma((2, NZ)), dma((NZ,)), dma((2, NZ)),
                dma((2, NZ)), dma((NZ,)),
                dma((2,)), dma((4, NH)), dma((2,)), dma((NZ,)), dma((NZ,)), dma, dma, dma,
            ],
            compiler_params=pltpu.CompilerParams(
                collective_id=0, has_side_effects=True, vmem_limit_bytes=60 << 20
            ),
        )(order, resp, q, k, v)
        return pl.pallas_call(
            finish,
            out_shape=(
                jax.ShapeDtypeStruct(out.shape, out.dtype),
                jax.ShapeDtypeStruct(lse.shape, lse.dtype),
            ),
            in_specs=[hbm, hbm],
            out_specs=(hbm, hbm),
            scratch_shapes=[
                pltpu.VMEM(out.shape, out.dtype),
                pltpu.VMEM(lse.shape, lse.dtype),
                dma((NB + 1,)),
                dma((NB + 1,)),
            ],
            compiler_params=pltpu.CompilerParams(vmem_limit_bytes=60 << 20),
        )(out, lse)

    rows = P(("dp", "ctx"), "head")
    return jax.shard_map(
        step,
        mesh=mesh,
        in_specs=(rows, rows, rows, P("dp"), P("dp")),
        out_specs=(P(("dp", "ctx"), "head", None), P("head", ("dp", "ctx"))),
        check_vma=False,
    )
```

```python
import functools
import math

import jax
import jax.numpy as jnp
from jax import lax
from jax.experimental import pallas as pl
from jax.experimental.pallas import tpu as pltpu
from jax.sharding import PartitionSpec as P

MESH = pl.DeviceIdType.MESH
D = 128
BLK = 128
NZ = 8
NH = 4
NB = 3
GROUP = 5
SUB = BLK // NH
NBLK = NZ * NB
PROMPT_BLOCKS = 6
BAND_BLOCKS = 8
ROWS = NB * SUB
WIDTH = GROUP * D
CHUNKS = ((0, 3), (3, 5))
SCALE = 1.0 / math.sqrt(D)
LOG2E = 1.4426950408889634
NEG = -1e30


def kernel(
    order_ref, resp_ref, q_ref, k_ref, v_ref, out_ref, lse_ref,
    vstage, qstage, kv, kseq, vseq, qbuf_a, qbuf_b, obuf, bias,
    lse_seq, lse_send, lse_recv, inv_ref,
    kv_send, v_send, q1_send, q2_send, x_send, c_send, o_send, l_send,
    v_recv, q1_recv, q2_recv, z_recv, x_recv, c_recv, o_recv, l_recv,
):
    z = lax.axis_index("ctx")
    h = lax.axis_index("head")
    x_peer = lax.rem(h + 2, NH)
    c_peer = h + 1 - 2 * lax.rem(h, 2)
    d_peer = lax.rem(c_peer + 2, NH)
    peers = (c_peer, x_peer, d_peer)
    qbuf = (qbuf_a, qbuf_b)

    def plane(k):
        return lax.rem(2 * k, NZ) + k // 4

    my_k = z // 2 + 4 * lax.rem(z, 2)
    my_src = my_k // 2

    barrier = pltpu.get_barrier_semaphore()
    for dz in (4, 3, 5, 2, 6, 1, 7):
        pl.semaphore_signal(
            barrier, inc=1, device_id={"ctx": lax.rem(z + dz, NZ)}, device_id_type=MESH
        )
    for th in peers:
        pl.semaphore_signal(barrier, inc=1, device_id={"head": th}, device_id_type=MESH)
    for kk in range(2):
        tz = plane(2 * h + kk)

        @pl.when(tz != z)
        def _():
            for th in peers:
                pl.semaphore_signal(
                    barrier, inc=1, device_id={"ctx": tz, "head": th}, device_id_type=MESH
                )

    pl.semaphore_wait(barrier, NZ - 1 + NH - 1 + jnp.where(my_src == h, 0, NZ - 1))

    def remote(src, dst, send_sem, recv_sem, tz, th):
        return pltpu.make_async_remote_copy(
            src, dst, send_sem, recv_sem, device_id={"ctx": tz, "head": th}, device_id_type=MESH
        )

    def send(src, dst, send_sem, recv_sem, tz, th=h):
        mine = (tz == z) & (th == h)

        @pl.when(mine)
        def _():
            pltpu.make_async_copy(src, dst, recv_sem).start()

        @pl.when(jnp.logical_not(mine))
        def _():
            remote(src, dst, send_sem, recv_sem, tz, th).start()

    def sent(src, dst, send_sem, recv_sem, tz, th=h):
        @pl.when(jnp.logical_not((tz == z) & (th == h)))
        def _():
            remote(src, dst, send_sem, recv_sem, tz, th).wait_send()

    def landed(ref, sem):
        pltpu.make_async_copy(ref, ref, sem).wait()

    here = pl.ds(NB * z, NB)

    k_moves = [
        (k_ref.at[:, :, pl.ds(D * kk, D)], kv.at[0, here], kv_send.at[kk], z_recv.at[z],
         plane(2 * h + kk))
        for kk in range(2)
    ]
    v_moves = [
        (vstage.at[:, :, pl.ds(D * kk, D)], kv.at[1, here], kv_send.at[2 + kk], z_recv.at[z],
         plane(2 * x_peer + kk))
        for kk in range(2)
    ]
    v1_moves = [
        (v_ref.at[:, :, pl.ds(D * kk, D)], vstage.at[:, :, pl.ds(D * kk, D)],
         v_send.at[kk], v_recv.at[kk], z, x_peer)
        for kk in range(2)
    ]
    for move in v1_moves:
        remote(*move).start()
    for move in k_moves:
        send(*move)

    def q_cols(c, kk):
        first, last = CHUNKS[c]
        return pl.ds(WIDTH * kk + D * first, D * (last - first))

    def q1_move(c, kk, e):
        rows = pl.ds(pl.multiple_of(SUB * peers[e], SUB), SUB)
        n = 2 * c + kk
        return (
            q_ref.at[:, rows, q_cols(c, kk)], qstage.at[h, :, :, q_cols(c, kk)],
            q1_send.at[n, e], q1_recv.at[n, h], z, peers[e],
        )

    q1_moves = [q1_move(c, kk, e) for c in range(2) for kk in range(2) for e in range(NH - 1)]

    def share_queries(c, *where):
        for e in where:
            for kk in range(2):
                remote(*q1_move(c, kk, e)).start()

    def q2_move(c, e, kk):
        hd = (h, *peers)[e]
        if e == 0:
            src = q_ref.at[:, pl.ds(pl.multiple_of(SUB * h, SUB), SUB), q_cols(c, kk)]
        else:
            src = qstage.at[hd, :, :, q_cols(c, kk)]
        return (
            src, qbuf[c].at[here], q2_send.at[c, 2 * e + kk], q2_recv.at[c], plane(2 * hd + kk),
        )

    q2_moves = [q2_move(c, e, kk) for c in range(2) for e in range(NH) for kk in range(2)]

    def forward(c, e):
        for kk in range(2):
            move = q2_move(c, e, kk)
            if e:
                landed(move[0], q1_recv.at[2 * c + kk, (h, *peers)[e]])
            send(*move)

    share_queries(0, 0)
    share_queries(1, 0)

    for kk in range(2):
        landed(v_moves[kk][0], v_recv.at[kk])
        send(*v_moves[kk])
    share_queries(0, 1, 2)
    forward(0, 0)
    forward(0, 1)

    def find(p, c):
        found = jnp.int32(0)
        for j in range(NBLK):
            found = jnp.where(order_ref[j] == p, j, found)
        inv_ref[p] = found
        return c

    lax.fori_loop(0, NBLK, find, 0)

    lane = lax.broadcasted_iota(jnp.int32, (ROWS, D), 1)
    row = lax.broadcasted_iota(jnp.int32, (ROWS, D), 0)
    row_pos = (row // SUB) * BLK + lax.rem(row, SUB) + SUB * h

    def band_start(o):
        return jnp.where(o < 2, 0, jnp.maximum(PROMPT_BLOCKS, NB * o - 5))

    def masks(o, c):
        q_pos = row_pos + o * (NB * BLK)
        start = jnp.full((ROWS, D), PROMPT_BLOCKS * BLK, jnp.int32)
        end = jnp.int32(PROMPT_BLOCKS * BLK)
        for n in range(resp_ref.shape[0]):
            end = end + resp_ref[n]
            start = jnp.where(q_pos >= end, end, start)
        start = jnp.where(o < 2, 0, start)
        for b in range(BAND_BLOCKS):
            key_pos = lane + (band_start(o) + b) * BLK
            allowed = (key_pos >= start) & (key_pos <= q_pos)
            bias[o, :, pl.ds(b * BLK, BLK)] = jnp.where(allowed, 0.0, NEG)
        return c

    lax.fori_loop(0, NZ, masks, 0)

    primary = lax.rem(h, 2) == lax.rem(my_src, 2)
    which = lax.rem(h // 2 + my_src // 2, 2)

    def piece(w, s):
        return kv.at[w, pl.ds(NB * s, NB)]

    def x_move(s):
        src = piece(which, s)
        return (src, src, x_send.at[s], x_recv.at[s], z, x_peer)

    def c_move(w, s):
        src = piece(w, s)
        return (src, src, c_send.at[w, s], c_recv, z, c_peer)

    def source(t):
        return lax.rem(z + 4 + ((t + 1) // 2) * (1 - 2 * lax.rem(t, 2)), NZ)

    @pl.when(primary)
    def _():
        def own(t, c):
            s = source(NZ - 1 - t)
            landed(piece(which, s), z_recv.at[s])
            remote(*x_move(s)).start()
            return c

        lax.fori_loop(0, NZ, own, 0)

    forward(0, 2)
    forward(0, 3)
    share_queries(1, 1, 2)
    forward(1, 0)
    forward(1, 1)

    @pl.when(primary)
    def _():
        def other(t, c):
            s = source(NZ - 1 - t)
            landed(piece(1 - which, s), x_recv.at[s])
            remote(*c_move(which, s)).start()
            remote(*c_move(1 - which, s)).start()
            return c

        lax.fori_loop(0, NZ, other, 0)

    forward(1, 2)
    forward(1, 3)

    @pl.when(jnp.logical_not(primary))
    def _():
        landed(kv, c_recv)

    def build(p, c):
        j = inv_ref[p]
        at = pl.ds(pl.multiple_of(p * BLK, BLK), BLK)
        kseq[:, at] = kv[0, j].T
        vseq[at, :] = kv[1, j]
        return c

    lax.fori_loop(0, NBLK, build, 0)

    out_col = my_k * WIDTH

    def o_move(c, o):
        first, last = CHUNKS[c]
        size = (last - first) * D
        cols = pl.ds(pl.multiple_of(out_col + first * D, D), size)
        src = obuf.at[o, :, :, pl.ds(first * D, size)]
        return (src, out_ref.at[:, :, cols], o_send.at[c, o], o_recv, o)

    def attend(c, o, spans):
        idx = [inv_ref[NB * o + b] for b in range(NB)]
        begin, end = CHUNKS[c]
        n = end - begin
        q = jnp.concatenate(
            [qbuf[c][j, :, pl.ds(g * D, D)] for g in range(n) for j in idx], axis=0
        )
        scores = []
        for at, use_bias in spans:
            s = jnp.dot(q, kseq[:, at], preferred_element_type=jnp.float32)
            if use_bias:
                mask = bias[o, :, pl.ds(0, s.shape[1])]
                s = (s.reshape(n, ROWS, -1) + mask[None]).reshape(s.shape)
            scores.append(s)
        top = functools.reduce(jnp.maximum, [jnp.max(s, axis=1, keepdims=True) for s in scores])
        total = jnp.zeros((n * ROWS, 1), jnp.float32)
        acc = jnp.zeros((n * ROWS, D), jnp.float32)
        for (at, _), s in zip(spans, scores):
            w = jnp.exp2((s - top) * (SCALE * LOG2E))
            total = total + jnp.sum(w, axis=1, keepdims=True)
            acc = acc + jnp.dot(
                w.astype(jnp.bfloat16), vseq[at, :], preferred_element_type=jnp.float32
            )
        res = (acc / total).astype(jnp.bfloat16)
        lse = top * SCALE + jnp.log(total)
        tile = jnp.zeros((ROWS, D), jnp.float32)
        for i in range(n):
            for b in range(NB):
                first = i * ROWS + b * SUB
                obuf[o, b, :, pl.ds((begin + i) * D, D)] = res[first : first + SUB]
            tile = jnp.where(lane == begin + i, lse[i * ROWS : (i + 1) * ROWS], tile)
        tile = jnp.concatenate([tile, jnp.zeros((D - ROWS, D), jnp.float32)], axis=0).T[:8]
        for b in range(NB):
            part = tile if b == 0 else pltpu.roll(tile, D - SUB * b, 1)
            lse_seq[NB * o + b] = part if c == 0 else part + lse_seq[NB * o + b]

    for c in range(2):
        landed(qbuf[c], q2_recv.at[c])

        def owner(t, carry, c=c):
            o = source(t)

            @pl.when(o < 2)
            def _():
                attend(c, o, [(pl.ds(0, PROMPT_BLOCKS * BLK), True)])

            @pl.when(o >= 2)
            def _():
                first = pl.multiple_of(band_start(o) * BLK, BLK)
                attend(c, o, [
                    (pl.ds(0, PROMPT_BLOCKS * BLK), False),
                    (pl.ds(first, BAND_BLOCKS * BLK), True),
                ])

            send(*o_move(c, o))
            return carry

        lax.fori_loop(0, NZ, owner, 0)

    lane8 = lax.broadcasted_iota(jnp.int32, (8, D), 1)

    def l_move(s):
        return (lse_send.at[s], lse_recv.at[h, lax.rem(my_k, 2)], l_send.at[s], l_recv, s, my_src)

    for s in range(NZ):
        tile = lse_seq[order_ref[NB * s]]
        for b in range(1, NB):
            tile = jnp.where(
                lane8 >= SUB * b, pltpu.roll(lse_seq[order_ref[NB * s + b]], SUB * b, 1), tile
            )
        lse_send[s] = tile
        send(*l_move(s))

    landed(lse_recv, l_recv)
    for kk in range(2):
        for b in range(NB):
            tile = jnp.zeros((8, D), jnp.float32)
            for r in range(NH):
                shift = (SUB * (r - b)) % D
                part = lse_recv[r, kk]
                part = pltpu.roll(part, shift, 1) if shift else part
                tile = jnp.where(lane8 >= SUB * r, part, tile)
            lse_ref[pl.ds(kk * GROUP, GROUP), pl.ds(b * BLK, BLK)] = tile[:GROUP]

    for move in v1_moves:
        remote(*move).wait_send()
    for move in k_moves + v_moves + q2_moves:
        sent(*move)
    for move in q1_moves:
        remote(*move).wait_send()

    @pl.when(primary)
    def _():
        def done(s, c):
            remote(*x_move(s)).wait_send()
            remote(*c_move(0, s)).wait_send()
            remote(*c_move(1, s)).wait_send()
            return c

        lax.fori_loop(0, NZ, done, 0)

    for s in range(NZ):
        sent(*l_move(jnp.int32(s)))
        for c in range(2):
            sent(*o_move(c, jnp.int32(s)))
    landed(out_ref, o_recv)


def finish(out_ref, lse_ref, out, lse, out_v, lse_v, sem, sem2):
    pairs = [(out_ref.at[b], out_v.at[b], out.at[b]) for b in range(NB)] + [(lse_ref, lse_v, lse)]
    ins = [pltpu.make_async_copy(p[0], p[1], sem.at[i]) for i, p in enumerate(pairs)]
    outs = [pltpu.make_async_copy(p[1], p[2], sem2.at[i]) for i, p in enumerate(pairs)]
    for copy in ins:
        copy.start()
    for i, o in zip(ins, outs):
        i.wait()
        o.start()
    for o in outs:
        o.wait()


def solution(mesh):
    def step(q, k, v, order, resp):
        q = q.reshape(NB, BLK, q.shape[1])
        k = k.reshape(NB, BLK, k.shape[1])
        v = v.reshape(NB, BLK, v.shape[1])
        smem = pl.BlockSpec(memory_space=pltpu.SMEM)
        hbm = pl.BlockSpec(memory_space=pl.ANY)
        vmem = pl.BlockSpec(memory_space=pltpu.VMEM)
        dma = pltpu.SemaphoreType.DMA
        bf16 = lambda *shape: pltpu.VMEM(shape, jnp.bfloat16)
        f32 = lambda *shape: pltpu.VMEM(shape, jnp.float32)
        out, lse = pl.pallas_call(
            kernel,
            out_shape=(
                jax.ShapeDtypeStruct((NB, SUB, NZ * WIDTH), jnp.bfloat16),
                jax.ShapeDtypeStruct((2 * GROUP, NB * BLK), jnp.float32),
            ),
            in_specs=[smem, smem, hbm, hbm, hbm],
            out_specs=(hbm, vmem),
            scratch_shapes=[
                bf16(NB, BLK, 2 * D),
                bf16(NH, NB, SUB, 2 * WIDTH),
                bf16(2, NBLK, BLK, D),
                bf16(D, NBLK * BLK),
                bf16(NBLK * BLK, D),
                *[bf16(NBLK, SUB, D * (last - first)) for first, last in CHUNKS],
                bf16(NZ, NB, SUB, WIDTH),
                f32(NZ, ROWS, BAND_BLOCKS * BLK),
                f32(NBLK, 8, D),
                f32(NZ, 8, D),
                f32(NH, 2, 8, D),
                pltpu.SMEM((NBLK,), jnp.int32),
                dma((4,)), dma((2,)), dma((4, NH - 1)), dma((2, NZ)), dma((NZ,)), dma((2, NZ)),
                dma((2, NZ)), dma((NZ,)),
                dma((2,)), dma((4, NH)), dma((2,)), dma((NZ,)), dma((NZ,)), dma, dma, dma,
            ],
            compiler_params=pltpu.CompilerParams(
                collective_id=0, has_side_effects=True, vmem_limit_bytes=60 << 20
            ),
        )(order, resp, q, k, v)
        return pl.pallas_call(
            finish,
            out_shape=(
                jax.ShapeDtypeStruct(out.shape, out.dtype),
                jax.ShapeDtypeStruct(lse.shape, lse.dtype),
            ),
            in_specs=[hbm, hbm],
            out_specs=(hbm, hbm),
            scratch_shapes=[
                pltpu.VMEM(out.shape, out.dtype),
                pltpu.VMEM(lse.shape, lse.dtype),
                dma((NB + 1,)),
                dma((NB + 1,)),
            ],
            compiler_params=pltpu.CompilerParams(vmem_limit_bytes=60 << 20),
        )(out, lse)

    rows = P(("dp", "ctx"), "head")
    return jax.shard_map(
        step,
        mesh=mesh,
        in_specs=(rows, rows, rows, P("dp"), P("dp")),
        out_specs=(P(("dp", "ctx"), "head", None), P("head", ("dp", "ctx"))),
        check_vma=False,
    )
```
